768 devices in a mesh: grp: 8 (over x, z_hi), fsdp: 16 (over y, core), seq: 6 (over z_lo).
Axes of the slice: x: 4, y: 8, z: 12 (z_hi: 2, z_lo: 6; z = z_hi * 6 + z_lo), core: 2. Of those that a mesh axis runs over, the one named last changes fastest.
Arguments:
- latents: bfloat16 [128, 768, 1536], P(('grp', 'fsdp'), 'seq'), may hold values from -6 to 6
- norm_gain: float32 [1536], replicated, may hold values from 0.1 to 1.9
- w_qkv: bfloat16 [3, 1536, 1536], P(None, ('grp', 'fsdp'), 'seq'), may hold values from -0.15625 to 0.15625
- w_out: bfloat16 [1536, 1536], P('seq', ('grp', 'fsdp')), may hold values from -0.15625 to 0.15625
- head_temp: float32 [24], P('seq'), may hold values from 0.5 to 40
- lengths: int32 [128], P(('grp', 'fsdp')), may hold values from 384 to 768, as said below
Outputs:
- attended: bfloat16 [128, 768, 1536], P(('grp', 'fsdp'), 'seq')
The draws below stay inside these ranges and needn't reach their ends.
Inputs may be any that keep to these rules, and one draw needn't show every extreme that they name: `lengths`: at least one clip has all 768 frames live.
All inputs are finite; a program needn't handle non-finite values.
Results may differ from the reference program's by a relative error of at most 0.02.
The reference program's roundings to bfloat16 on the way count: a program that leaves them out, or rounds other values in their place, can miss the bound.
Values may be sent and summed in bfloat16 or wider, within the bound.
No kernel may reach another device: no remote copies, remote signals or barrier semaphores. Data moves between devices by JAX's collectives and lax.ppermute only.
A program may use at most 64 MiB of HBM per device.

```python
import jax
import jax.numpy as jnp
from jax import lax

D = 1536
HEADS = 24
HD = 64
LEN = 768
CLIPS = 128


def draw_head_temp(key, part):
    spread = jax.random.uniform(key, (HEADS,), jnp.float32)
    return 0.5 * jnp.exp(spread * jnp.log(4.0))


def draw_lengths(key, part):
    first, second = jax.random.split(key)
    values = jax.random.randint(first, (CLIPS,), LEN // 2, LEN + 1)
    chosen = jax.random.randint(second, (), 0, CLIPS)
    return jnp.where(jnp.arange(CLIPS) == chosen, LEN, values).astype(jnp.int32)


def level_of(rng, shape, cuts, low, high):
    level = 1.0
    for axis_at, shards_of in cuts:
        draws = jax.random.uniform(jax.random.fold_in(jax.random.fold_in(rng, 6), axis_at), (shards_of,), jnp.float32, low / len(cuts), high / len(cuts))
        level = level * jnp.repeat(jnp.exp(draws), shape[axis_at] // shards_of).reshape((-1,) + (1,) * (len(shape) - 1 - axis_at))
    return level


def bell_draw(own_key, dims, width, limit, cuts=(), kind=jnp.bfloat16):
    factor_of = level_of(own_key, dims, cuts, -0.22, 0.18) if cuts else 1.0
    result = jax.random.normal(own_key, dims, jnp.float32) * width * factor_of
    return jnp.minimum(jnp.maximum(result, -limit), limit).astype(kind)


def setup_inputs(seed: int = 0) -> dict:
    keys = jax.random.split(jax.random.key(seed), 7)
    latents = bell_draw(keys[0], (CLIPS, LEN, D), 1.0, 6.0, ((0, 128), (1, 6)))
    norm_gain = jnp.clip(1.0 + 0.18 * jax.random.normal(keys[1], (D,), jnp.float32), 0.1, 1.9)
    w_qkv = bell_draw(keys[2], (3, D, D), D ** -0.5, 0.15625, ((1, 128), (2, 6)))
    w_out = bell_draw(keys[3], (D, D), D ** -0.5, 0.15625, ((0, 6), (1, 128)))
    head_temp = draw_head_temp(jax.random.fold_in(keys[6], 71), 0)
    lengths = draw_lengths(jax.random.fold_in(keys[6], 71), 0)
    return dict(latents=latents, norm_gain=norm_gain, w_qkv=w_qkv, w_out=w_out, head_temp=head_temp, lengths=lengths)


def one_clip(args):
    clip, gain, w_qkv, w_out, head_temp, length = args
    values = clip.astype(jnp.float32)
    rms = jnp.sqrt(lax.optimization_barrier(jnp.mean(values * values, axis=-1, keepdims=True)) + 1e-06)
    normed = (values / rms * gain).astype(jnp.bfloat16)
    query = jnp.dot(normed, w_qkv[0], preferred_element_type=jnp.float32).astype(jnp.bfloat16)
    key_part = jnp.dot(normed, w_qkv[1], preferred_element_type=jnp.float32).astype(jnp.bfloat16)
    value = jnp.dot(normed, w_qkv[2], preferred_element_type=jnp.float32).astype(jnp.bfloat16)
    query = query.reshape(LEN, HEADS, HD).astype(jnp.float32)
    key_part = key_part.reshape(LEN, HEADS, HD).astype(jnp.float32)
    value = value.reshape(LEN, HEADS, HD).astype(jnp.float32)
    scores = jnp.einsum('qhd,khd->hqk', query, key_part) * (head_temp / 8.0)[:, None, None]
    live = jnp.arange(LEN, dtype=jnp.int32) < length
    scores = jnp.where(live[None, None, :], scores, -1e+30)
    probs = jax.nn.softmax(scores, axis=-1).astype(jnp.bfloat16)
    heads_out = jnp.einsum('hqk,khd->qhd', probs.astype(jnp.float32), value).astype(jnp.bfloat16)
    heads_out = heads_out.reshape(LEN, D)
    return jnp.dot(heads_out, w_out, preferred_element_type=jnp.float32).astype(jnp.bfloat16)

def reference(latents, norm_gain, w_qkv, w_out, head_temp, lengths):

    def step(pair):
        clip, length = pair
        return one_clip((clip, norm_gain, w_qkv, w_out, head_temp, length))
    return lax.map(step, (latents, lengths))
```

```python
import jax
import jax.numpy as jnp
import numpy as np
from jax import lax
from jax.sharding import Mesh, PartitionSpec as P

HD = 64
AXES = ("x", "zh", "y", "c", "zl")
SIZES = (4, 2, 8, 2, 6)


def index_of(x, zh, y, c, zl):
    return (((x * 2 + zh) * 8 + y) * 2 + c) * 6 + zl


def permute(value, move):
    nx, nh, ny, nc, nl = SIZES
    pairs = [
        (index_of(x, zh, y, c, zl), index_of(*move(x, zh, y, c, zl)))
        for x in range(nx)
        for zh in range(nh)
        for y in range(ny)
        for c in range(nc)
        for zl in range(nl)
    ]
    return lax.ppermute(value, AXES, pairs)


def other_half(value):
    return permute(value, lambda x, zh, y, c, zl: (x, 1 - zh, y, c, zl))


def other_core(value):
    return permute(value, lambda x, zh, y, c, zl: (x, zh, y, 1 - c, zl))


def y_shift(value, step):
    return permute(value, lambda x, zh, y, c, zl: (x, zh, (y + step) % 8, c, zl))


def gather_by_exchange(value, axes, count):
    copies = jnp.broadcast_to(value[None], (count,) + value.shape)
    return lax.all_to_all(copies, axes, 0, 0, tiled=True)


def pair(own, other, axis):
    first = lax.axis_index(axis) == 0
    return jnp.stack([jnp.where(first, own, other), jnp.where(first, other, own)])


def gather_y_ring(value):
    y = lax.axis_index("y")
    whole = jnp.zeros((8,) + value.shape, value.dtype)

    def put(buffer, block, distance):
        return lax.dynamic_update_slice_in_dim(buffer, block[None], lax.rem(y + distance, 8), 0)

    up = down = value
    whole = put(whole, value, 0)
    for step in range(1, 5):
        up = y_shift(up, 1)
        whole = put(whole, up, 8 - step)
        if step < 4:
            down = y_shift(down, -1)
            whole = put(whole, down, step)
    return whole


def feature_at():
    c, y, x, zh, r = np.meshgrid(
        np.arange(2), np.arange(8), np.arange(4), np.arange(2), np.arange(12), indexing="ij"
    )
    return ((((x * 2 + zh) * 8 + y) * 2 + c) * 12 + r).reshape(-1).astype(np.int32)


def whole_w_qkv(w_qkv):
    rows = w_qkv.transpose(1, 0, 2).reshape(12, 768)
    halves = pair(rows, other_half(rows), "zh").reshape(24, 768)
    by_x = gather_by_exchange(halves, "x", 4)
    by_y = gather_y_ring(by_x.reshape(96, 768))
    by_core = pair(by_y, other_core(by_y), "c").reshape(1536, 768)
    place = jnp.asarray(feature_at())
    chosen = (jnp.arange(1536, dtype=jnp.int32)[:, None] == place[None, :]).astype(jnp.bfloat16)
    return jnp.dot(chosen, by_core, preferred_element_type=jnp.float32).astype(jnp.bfloat16)


def half_w_out(w_out):
    turned = w_out.T
    by_z = gather_by_exchange(turned, ("zh", "zl"), 12)
    rows = by_z.reshape(2, 6, 12, 256).transpose(0, 2, 1, 3).reshape(24, 1536)
    by_x = gather_by_exchange(rows, "x", 4)
    return lax.all_gather(by_x.reshape(96, 1536), "y", axis=0, tiled=True)


def project_out(heads_out, own_rows, other_rows):
    place = jnp.asarray(feature_at()[:768])
    core = lax.axis_index("c")
    total = 0.0
    for rows, at in ((own_rows, core), (other_rows, 1 - core)):
        part = lax.dot_general(
            heads_out, rows, (((1,), (1,)), ((), ())), preferred_element_type=jnp.float32
        ).astype(jnp.bfloat16)
        chosen = (place[:, None] + at * 12 == jnp.arange(1536, dtype=jnp.int32)[None, :]).astype(
            jnp.bfloat16
        )
        total = total + jnp.dot(part, chosen, preferred_element_type=jnp.float32)
    return total.astype(jnp.bfloat16)


def on_device(latents, norm_gain, w_qkv, w_out, head_temp, lengths):
    frames = latents[0]
    values = frames.astype(jnp.float32)
    rms = jnp.sqrt(jnp.mean(values * values, axis=-1, keepdims=True) + 1e-06)
    normed = (values / rms * norm_gain).astype(jnp.bfloat16)
    whole = lax.all_gather(normed, "zl", axis=0, tiled=True)
    total_rows = whole.shape[0]
    local_width = w_qkv.shape[2]
    local_heads = local_width // HD
    weights = lax.optimization_barrier(whole_w_qkv(w_qkv))
    own_rows = half_w_out(w_out)
    projected = jnp.dot(whole, weights, preferred_element_type=jnp.float32).astype(jnp.bfloat16)
    query, key_part, value = (
        projected[:, k * local_width : (k + 1) * local_width].reshape(total_rows, local_heads, HD)
        for k in range(3)
    )
    scores = jnp.einsum("qhd,khd->hqk", query, key_part, preferred_element_type=jnp.float32)
    scores = scores * (head_temp / 8.0)[:, None, None]
    live = jnp.arange(total_rows, dtype=jnp.int32) < lengths[0]
    scores = jnp.where(live[None, None, :], scores, -1e30)
    probs = jax.nn.softmax(scores, axis=-1).astype(jnp.bfloat16)
    heads_out = jnp.einsum("hqk,khd->qhd", probs, value, preferred_element_type=jnp.float32).astype(
        jnp.bfloat16
    )
    heads_out, own_rows = lax.optimization_barrier((heads_out, own_rows))
    other_rows = other_core(own_rows)
    blocks = heads_out.reshape(6, total_rows // 6, local_width)
    own = lax.all_to_all(blocks, "zl", 0, 0, tiled=True)
    own = own.transpose(1, 0, 2).reshape(total_rows // 6, 6 * local_width)
    attended = project_out(own, own_rows, other_rows)
    return attended[None]


def solution(mesh):
    split = Mesh(mesh.devices.reshape(SIZES), AXES)
    clip = ("x", "zh", "y", "c")
    in_specs = (
        P(clip, "zl", None),
        P(),
        P(None, clip, "zl"),
        P("zl", clip),
        P("zl"),
        P(clip),
    )
    out_specs = P(clip, "zl", None)
    return jax.shard_map(
        on_device, mesh=split, in_specs=in_specs, out_specs=out_specs, check_vma=False
    )
```

```python
import jax
import jax.numpy as jnp
import numpy as np
from jax import lax
from jax.sharding import Mesh, PartitionSpec as P

HD = 64
AXES = ("x", "zh", "y", "c", "zl")
SIZES = (4, 2, 8, 2, 6)


def permute(value, move):
    pairs = []
    for place in np.ndindex(*SIZES):
        goal = move(*place)
        if goal is not None:
            pairs.append(
                (int(np.ravel_multi_index(place, SIZES)), int(np.ravel_multi_index(goal, SIZES)))
            )
    return lax.ppermute(value, AXES, pairs)


def other_core(value):
    return permute(value, lambda x, zh, y, c, zl: (x, zh, y, 1 - c, zl))


def z_shift(value, step):
    return permute(
        value,
        lambda x, zh, y, c, zl: (x, zh, y, c, zl + step) if 0 <= zl + step < 6 else None,
    )


def gather_by_exchange(value, axes, count):
    copies = jnp.broadcast_to(value[None], (count,) + value.shape)
    return lax.all_to_all(copies, axes, 0, 0, tiled=True)


def after(value, *others):
    return lax.optimization_barrier((value,) + others)[0]


def relay_frames(shard):
    ups, downs = [shard], [shard]
    for _ in range(5):
        ups.append(z_shift(ups[-1], 1))
        downs.append(z_shift(downs[-1], -1))
    return ups, downs


def in_order(ups, downs):
    place = lax.axis_index("zl")
    whole = jnp.zeros((6,) + ups[0].shape, ups[0].dtype)
    whole = lax.dynamic_update_slice_in_dim(whole, ups[0][None], place, 0)
    for ahead in range(1, 6):
        block = jnp.where(place + ahead <= 5, downs[ahead], ups[6 - ahead])
        whole = lax.dynamic_update_slice_in_dim(whole, block[None], lax.rem(place + ahead, 6), 0)
    return whole.reshape(-1, whole.shape[-1])


def by_place(own, other, axis):
    first = lax.axis_index(axis) == 0
    return jnp.where(first, own, other), jnp.where(first, other, own)


def apart_shift(value):
    return permute(
        value, lambda x, zh, y, c, zl: (x, zh, (y + 1 - 2 * c) % 8, c, zl)
    )


def stack_by_y(own, other):
    y = lax.axis_index("y")
    turn = 1 - 2 * lax.axis_index("c")
    whole = jnp.zeros((8,) + own[0].shape, own[0].dtype)
    for step, block in enumerate(own):
        at = lax.rem(y - turn * step + 8, 8)
        whole = lax.dynamic_update_slice_in_dim(whole, block[None], at, 0)
    for step in range(1, 4):
        at = lax.rem(y + turn * step + 8, 8)
        whole = lax.dynamic_update_slice_in_dim(whole, other[step - 1][None], at, 0)
    return whole


def stack_by_x(own, below, above, across):
    x = lax.axis_index("x")
    whole = jnp.zeros((4,) + own.shape, own.dtype)
    for step, block in ((0, own), (3, below), (1, above), (2, across)):
        whole = lax.dynamic_update_slice_in_dim(whole, block[None], lax.rem(x + step, 4), 0)
    return whole


def x_shift(value, step):
    return permute(value, lambda x, zh, y, c, zl: ((x + step) % 4, zh, y, c, zl))


def on_device(latents, norm_gain, w_qkv, w_out, head_temp, lengths):
    frames = latents[0]
    values = frames.astype(jnp.float32)
    rms = jnp.sqrt(jnp.mean(values * values, axis=-1, keepdims=True) + 1e-06)
    normed = (values / rms * norm_gain).astype(jnp.bfloat16)
    ups, downs = relay_frames(normed)

    rows = w_qkv.transpose(1, 0, 2).reshape(12, 768)
    rows = jnp.concatenate(by_place(rows, other_core(rows), "c"))
    by_x = gather_by_exchange(after(rows, normed), ("x", "zh"), 8)
    block = by_x.reshape(192, 768)
    steps = [block]
    for step in range(1, 5):
        ready = steps[-1]
        if step == 2:
            ready = after(ready, ups[2], downs[2])
        if step == 4:
            ready = after(ready, ups[3], downs[3])
        steps.append(apart_shift(ready))
    others = other_core(after(jnp.stack(steps[1:4]), ups[4], downs[4]))
    by_y = stack_by_y(steps, others).reshape(8, 8, 24, 768)
    weights = lax.optimization_barrier(by_y.transpose(1, 0, 2, 3).reshape(1536, 768))

    by_z = gather_by_exchange(after(w_out.T, steps[1]), ("zh", "zl"), 12)
    by_z = by_z.reshape(2, 2, 3, 12, 256)
    mine, given = by_place(by_z[:, 0], by_z[:, 1], "c")
    first, second = by_place(mine, other_core(given), "c")
    columns = jnp.stack([first, second], axis=1)
    columns = columns.transpose(0, 1, 3, 2, 4).reshape(48, 768)
    out_by_y = gather_by_exchange(after(columns, steps[2]), "y", 8).reshape(384, 768)
    out_by_y = after(out_by_y, ups[5], downs[5], others)
    out_by_x = stack_by_x(
        out_by_y, x_shift(out_by_y, 1), x_shift(out_by_y, 3), x_shift(out_by_y, 2)
    )

    whole = in_order(ups, downs)
    total_rows = whole.shape[0]
    local_width = w_qkv.shape[2]
    local_heads = local_width // HD
    projected = jnp.dot(whole, weights, preferred_element_type=jnp.float32).astype(jnp.bfloat16)
    query, key_part, value = (
        projected[:, k * local_width : (k + 1) * local_width].reshape(total_rows, local_heads, HD)
        for k in range(3)
    )
    scores = jnp.einsum("qhd,khd->hqk", query, key_part, preferred_element_type=jnp.float32)
    scores = scores * (head_temp / 8.0)[:, None, None]
    live = jnp.arange(total_rows, dtype=jnp.int32) < lengths[0]
    scores = jnp.where(live[None, None, :], scores, -1e30)
    probs = jax.nn.softmax(scores, axis=-1).astype(jnp.bfloat16)
    heads_out = jnp.einsum("hqk,khd->qhd", probs, value, preferred_element_type=jnp.float32).astype(
        jnp.bfloat16
    )
    blocks = heads_out.reshape(6, total_rows // 6, local_width)
    own = lax.all_to_all(blocks, "zl", 0, 0, tiled=True)
    out_own = out_by_x.reshape(4, 8, 2, 24, 768).transpose(0, 2, 1, 3, 4).reshape(1536, 768)
    out_other = other_core(after(out_own, blocks))
    own, out_own, out_other = lax.optimization_barrier((own, out_own, out_other))
    own = own.transpose(1, 0, 2).reshape(total_rows // 6, 6 * local_width)
    half = 3 * local_width
    mine, given = by_place(own[:, :half], own[:, half:], "c")
    attended = sum(
        lax.dot_general(part, rows, (((1,), (1,)), ((), ())), preferred_element_type=jnp.float32)
        for part, rows in ((mine, out_own), (given, out_other))
    ).astype(jnp.bfloat16)
    return attended[None]


def solution(mesh):
    split = Mesh(mesh.devices.reshape(SIZES), AXES)
    clip = ("x", "zh", "y", "c")
    in_specs = (
        P(clip, "zl", None),
        P(),
        P(None, clip, "zl"),
        P("zl", clip),
        P("zl"),
        P(clip),
    )
    out_specs = P(clip, "zl", None)
    return jax.shard_map(
        on_device, mesh=split, in_specs=in_specs, out_specs=out_specs, check_vma=False
    )
```

```python
import functools

import jax
import jax.numpy as jnp
import numpy as np
from jax import lax
from jax.experimental import pallas as pl
from jax.experimental.pallas import tpu as pltpu
from jax.sharding import Mesh, PartitionSpec as P

HD = 64
AXES = ("x", "zh", "y", "c", "zl")
SIZES = (4, 2, 8, 2, 6)


def permute(value, move):
    pairs = []
    for place in np.ndindex(*SIZES):
        goal = move(*place)
        if goal is not None:
            pairs.append(
                (int(np.ravel_multi_index(place, SIZES)), int(np.ravel_multi_index(goal, SIZES)))
            )
    return lax.ppermute(value, AXES, pairs)


def other_core(value):
    return permute(value, lambda x, zh, y, c, zl: (x, zh, y, 1 - c, zl))


def even_links(value):
    return permute(value, lambda x, zh, y, c, zl: (x, zh, y, c, zl ^ 1))


def odd_links(value):
    return permute(
        value, lambda x, zh, y, c, zl: (x, zh, y, c, ((zl - 1) ^ 1) + 1) if 0 < zl < 5 else None
    )


def x_swap(value, which):
    goal = {"even": (1, 0, 3, 2), "odd": (3, 2, 1, 0), "across": (2, 3, 0, 1)}[which]
    return permute(value, lambda x, zh, y, c, zl: (goal[x], zh, y, c, zl))


def gather_y(value):
    copies = jnp.broadcast_to(value[None], (8,) + value.shape)
    return lax.all_to_all(copies, "y", 0, 0, tiled=True).reshape(-1, value.shape[1])


def after(value, *others):
    return lax.optimization_barrier((value,) + others)[0]


def gather_x(block):
    return jnp.stack([block] + [x_swap(block, which) for which in ("even", "odd", "across")])


def x_places(x):
    return x, x + 1 - 2 * lax.rem(x, 2), 3 - x, lax.rem(x + 2, 4)


def reorder():
    y, zh, r = np.meshgrid(np.arange(8), np.arange(2), np.arange(24), indexing="ij")
    matrix = np.zeros((384, 384), np.float32)
    matrix[np.arange(384), ((zh * 8 + y) * 24 + r).reshape(-1)] = 1
    return jnp.asarray(matrix, jnp.bfloat16)


def attend_kernel(place_ref, length_ref, temp_ref, *refs):
    frames, weights_hbm, move_ref, out_ref = refs[:11], refs[11:13], refs[13], refs[14]
    x_buf, w_in, w_buf, qkv, sems = refs[15:]
    place, x, core = place_ref[0], place_ref[1], place_ref[2]
    turn = 1 - 2 * lax.rem(place, 2)

    pieces = [(frames[0], place, None)]
    for step in range(1, 6):
        for ref, at in (
            (frames[step], place + turn * step),
            (frames[5 + step], place - turn * step),
        ):
            pieces.append((ref, at, (at >= 0) & (at <= 5)))

    copies = [
        pltpu.make_async_copy(ref, x_buf.at[at], sems.at[number])
        for number, (ref, at, _) in enumerate(pieces)
    ]
    w_copies = [
        pltpu.make_async_copy(weights_hbm[which], w_in.at[which], sems.at[11 + which])
        for which in range(2)
    ]
    for copy in w_copies:
        copy.start()
    for copy, (_, _, valid) in zip(copies, pieces):
        if valid is None:
            copy.start()
        else:
            pl.when(valid)(copy.start)

    for copy in w_copies:
        copy.wait()
    for which, half in ((0, core), (1, 1 - core)):
        for number, at in enumerate(x_places(x)):
            rows = pl.ds(pl.multiple_of(at * 384, 384), 384)
            w_buf[half, rows, :] = lax.dot_general(
                move_ref[...],
                w_in[which, number],
                (((0,), (0,)), ((), ())),
                preferred_element_type=jnp.float32,
            ).astype(jnp.bfloat16)
    for copy, (_, _, valid) in zip(copies, pieces):
        if valid is None:
            copy.wait()
        else:
            pl.when(valid)(copy.wait)

    total = x_buf.shape[0] * x_buf.shape[1]
    for two in range(2):
        qkv[two] = jnp.dot(
            x_buf[...].reshape(total, x_buf.shape[2]),
            w_buf[two],
            preferred_element_type=jnp.float32,
        ).astype(jnp.bfloat16)

    live = lax.broadcasted_iota(jnp.int32, (1, total), 1) < length_ref[0]
    lane = lax.broadcasted_iota(jnp.int32, (128, 128), 1)
    row = lax.broadcasted_iota(jnp.int32, (256, 1), 0)

    def query_block(block, carry):
        rows = pl.ds(pl.multiple_of(block * 128, 128), 128)
        for two in range(2):
            query = qkv[two, rows, :128]
            none = jnp.zeros_like(query)
            query = jnp.concatenate(
                [jnp.where(lane < HD, query, none), jnp.where(lane < HD, none, query)]
            )
            scores = lax.dot_general(
                query,
                qkv[two, :, 128:256],
                (((1,), (1,)), ((), ())),
                preferred_element_type=jnp.float32,
            )
            scale = jnp.where(row < 128, temp_ref[2 * two] / 8.0, temp_ref[2 * two + 1] / 8.0)
            scores = jnp.where(live, scores * scale, -1e30)
            scores = jnp.exp(scores - jnp.max(scores, axis=-1, keepdims=True))
            probs = scores * (1.0 / jnp.sum(scores, axis=-1, keepdims=True))
            mixed = jnp.dot(
                probs.astype(jnp.bfloat16), qkv[two, :, 256:], preferred_element_type=jnp.float32
            )
            mixed = jnp.where(lane < HD, mixed[:128], mixed[128:])
            out_ref[block, :, two * 128 : two * 128 + 128] = mixed.astype(jnp.bfloat16)
        return carry

    lax.fori_loop(0, 6, query_block, 0)


SMEM = pl.BlockSpec(memory_space=pltpu.SMEM)
VMEM = pl.BlockSpec(memory_space=pltpu.VMEM)
ANYWHERE = pl.BlockSpec(memory_space=pl.ANY)


def attend(place, length, temp, frames, weights):
    shard = frames[0].shape
    return pl.pallas_call(
        attend_kernel,
        out_shape=jax.ShapeDtypeStruct((6, shard[0], 256), jnp.bfloat16),
        in_specs=[SMEM] * 3 + [ANYWHERE] * 13 + [VMEM],
        out_specs=VMEM,
        scratch_shapes=[
            pltpu.VMEM((6,) + shard, jnp.bfloat16),
            pltpu.VMEM((2, 4, 384, 384), jnp.bfloat16),
            pltpu.VMEM((2, 1536, 384), jnp.bfloat16),
            pltpu.VMEM((2, 6 * shard[0], 384), jnp.bfloat16),
            pltpu.SemaphoreType.DMA((13,)),
        ],
        compiler_params=pltpu.CompilerParams(vmem_limit_bytes=28 * 2**20),
        cost_estimate=pl.CostEstimate(
            flops=3 * 10**9, bytes_accessed=5 * 10**6, transcendentals=2 * 10**6
        ),
    )(place, length, temp, *frames, *weights, reorder())


def project_kernel(place_ref, heads_ref, own_ref, other_ref, move_ref, out_ref):
    x, core = place_ref[1], place_ref[2]
    first = jnp.concatenate([heads_ref[at, :, :128] for at in range(6)], axis=1)
    second = jnp.concatenate([heads_ref[at, :, 128:] for at in range(6)], axis=1)
    mine = jnp.where(core == 0, first, second)
    given = jnp.where(core == 0, second, first)
    sides = (((1,), (1,)), ((), ()))
    for number, at in enumerate(x_places(x)):
        columns = pl.ds(pl.multiple_of(at * 384, 384), 384)
        total = lax.dot_general(
            mine, own_ref[number], sides, preferred_element_type=jnp.float32
        ) + lax.dot_general(given, other_ref[number], sides, preferred_element_type=jnp.float32)
        out_ref[:, columns] = jnp.dot(
            total.astype(jnp.bfloat16), move_ref[...], preferred_element_type=jnp.float32
        ).astype(jnp.bfloat16)


def project(place, heads, own, other):
    return pl.pallas_call(
        project_kernel,
        out_shape=jax.ShapeDtypeStruct((heads.shape[1], 1536), jnp.bfloat16),
        in_specs=[SMEM] + [VMEM] * 4,
        out_specs=VMEM,
        compiler_params=pltpu.CompilerParams(vmem_limit_bytes=20 * 2**20),
        cost_estimate=pl.CostEstimate(
            flops=8 * 10**8, bytes_accessed=6 * 10**6, transcendentals=0
        ),
    )(place, heads, own, other, reorder())


def on_device(latents, norm_gain, w_qkv, w_out, head_temp, lengths):
    rows = w_qkv.reshape(3, 12, 2, 128).transpose(2, 1, 0, 3).reshape(1, 2, 12, 384)
    rows = jnp.broadcast_to(rows, (2, 2, 12, 384)).reshape(4, 12, 384)
    rows = lax.all_to_all(rows, ("zh", "c"), 0, 0, tiled=True).reshape(48, 384)

    frames = latents[0]
    values = frames.astype(jnp.float32)
    rms = jnp.sqrt(jnp.mean(values * values, axis=-1, keepdims=True) + 1e-06)
    normed = (values / rms * norm_gain).astype(jnp.bfloat16)
    evens, odds = [normed], [normed]
    for _ in range(5):
        even, odd = even_links(odds[-1]), odd_links(evens[-1])
        evens.append(even)
        odds.append(odd)

    by_y = gather_y(after(rows, normed))
    by_x = gather_x(after(by_y, evens[1], odds[1]))

    turned = w_out.T.reshape(1, 12, 2, 128).transpose(0, 2, 1, 3)
    turned = jnp.broadcast_to(turned, (12, 2, 12, 128)).reshape(2, 6, 2, 12, 128)
    turned = turned.reshape(24, 12, 128)
    columns = lax.all_to_all(after(turned, by_y), ("zh", "zl", "c"), 0, 0, tiled=True)
    columns = columns.reshape(2, 6, 2, 12, 128).transpose(0, 2, 3, 1, 4).reshape(48, 768)
    out_by_y = gather_y(after(columns, evens[2], odds[2]))

    weights = (by_x, other_core(after(by_x, evens[3], odds[3])))
    out_own = gather_x(after(out_by_y, evens[4], odds[4]))

    place = jnp.stack([lax.axis_index(axis) for axis in ("zl", "x", "c")]).astype(jnp.int32)
    blocks = attend(place, lengths, head_temp, evens + odds[1:], weights)
    own = lax.all_to_all(blocks, "zl", 0, 0, tiled=True)
    out_other = other_core(after(out_own, blocks))
    return project(place, own, out_own, out_other)[None]


def solution(mesh):
    split = Mesh(mesh.devices.reshape(SIZES), AXES)
    clip = ("x", "zh", "y", "c")
    in_specs = (
        P(clip, "zl", None),
        P(),
        P(None, clip, "zl"),
        P("zl", clip),
        P("zl"),
        P(clip),
    )
    out_specs = P(clip, "zl", None)
    return jax.shard_map(
        on_device, mesh=split, in_specs=in_specs, out_specs=out_specs, check_vma=False
    )
```

```python
import functools

import jax
import jax.numpy as jnp
import numpy as np
from jax import lax
from jax.experimental import pallas as pl
from jax.experimental.pallas import tpu as pltpu
from jax.sharding import Mesh, PartitionSpec as P

HD = 64
AXES = ("x", "zh", "y", "c", "zl")
SIZES = (4, 2, 8, 2, 6)


def permute(value, move):
    pairs = []
    for place in np.ndindex(*SIZES):
        goal = move(*place)
        if goal is not None:
            pairs.append(
                (int(np.ravel_multi_index(place, SIZES)), int(np.ravel_multi_index(goal, SIZES)))
            )
    return lax.ppermute(value, AXES, pairs)


def other_core(value):
    return permute(value, lambda x, zh, y, c, zl: (x, zh, y, 1 - c, zl))


def other_triple(value):
    return permute(value, lambda x, zh, y, c, zl: (x, zh, y, c, (zl + 3) % 6))


def triple_shift(value, step):
    return permute(
        value, lambda x, zh, y, c, zl: (x, zh, y, c, zl // 3 * 3 + (zl + step) % 3)
    )


def x_swap(value, which):
    goal = {"even": (1, 0, 3, 2), "odd": (3, 2, 1, 0), "across": (2, 3, 0, 1)}[which]
    return permute(value, lambda x, zh, y, c, zl: (goal[x], zh, y, c, zl))


def gather_y(value):
    copies = jnp.broadcast_to(value[None], (8,) + value.shape)
    return lax.all_to_all(copies, "y", 0, 0, tiled=True).reshape(-1, value.shape[1])


def after(value, *others):
    return lax.optimization_barrier((value,) + others)[0]


def gather_x(block):
    return [block] + [x_swap(block, which) for which in ("even", "odd", "across")]


def x_places(x):
    return x, x + 1 - 2 * lax.rem(x, 2), 3 - x, lax.rem(x + 2, 4)


def reorder():
    y, zh, r = np.meshgrid(np.arange(8), np.arange(2), np.arange(24), indexing="ij")
    matrix = np.zeros((384, 384), np.float32)
    matrix[np.arange(384), ((zh * 8 + y) * 24 + r).reshape(-1)] = 1
    return jnp.asarray(matrix, jnp.bfloat16)


def attend_kernel(place_ref, length_ref, temp_ref, *refs):
    frames, weights, move_ref, out_ref = refs[:6], refs[6:14], refs[14], refs[15]
    x_buf, w_in, w_buf, qkv, sems = refs[16:]
    place, x, core = place_ref[0], place_ref[1], place_ref[2]
    base, within = place // 3 * 3, lax.rem(place, 3)
    below, above = lax.rem(within + 2, 3), lax.rem(within + 1, 3)
    slots = (
        place,
        base + below,
        base + above,
        3 - base + within,
        3 - base + below,
        3 - base + above,
    )
    w_copies = [
        pltpu.make_async_copy(ref, w_in.at[number], sems.at[6 + number])
        for number, ref in enumerate(weights)
    ]
    copies = [
        pltpu.make_async_copy(ref, x_buf.at[at], sems.at[number])
        for number, (ref, at) in enumerate(zip(frames, slots))
    ]
    for copy in w_copies + copies:
        copy.start()
    for which, half in ((0, core), (1, 1 - core)):
        for number, at in enumerate(x_places(x)):
            w_copies[4 * which + number].wait()
            rows = pl.ds(pl.multiple_of(at * 384, 384), 384)
            w_buf[half, rows, :] = lax.dot_general(
                move_ref[...],
                w_in[4 * which + number],
                (((0,), (0,)), ((), ())),
                preferred_element_type=jnp.float32,
            ).astype(jnp.bfloat16)
    for copy in copies:
        copy.wait()

    total = x_buf.shape[0] * x_buf.shape[1]
    for two in range(2):
        qkv[two] = jnp.dot(
            x_buf[...].reshape(total, x_buf.shape[2]),
            w_buf[two],
            preferred_element_type=jnp.float32,
        ).astype(jnp.bfloat16)

    live = lax.broadcasted_iota(jnp.int32, (1, total), 1) < length_ref[0]
    lane = lax.broadcasted_iota(jnp.int32, (128, 128), 1)
    row = lax.broadcasted_iota(jnp.int32, (256, 1), 0)

    def query_block(block, carry):
        rows = pl.ds(pl.multiple_of(block * 128, 128), 128)
        for two in range(2):
            query = qkv[two, rows, :128]
            none = jnp.zeros_like(query)
            query = jnp.concatenate(
                [jnp.where(lane < HD, query, none), jnp.where(lane < HD, none, query)]
            )
            scores = lax.dot_general(
                query,
                qkv[two, :, 128:256],
                (((1,), (1,)), ((), ())),
                preferred_element_type=jnp.float32,
            )
            scale = jnp.where(row < 128, temp_ref[2 * two] / 8.0, temp_ref[2 * two + 1] / 8.0)
            scores = jnp.where(live, scores * scale, -1e30)
            scores = jnp.exp(scores - jnp.max(scores, axis=-1, keepdims=True))
            probs = scores * (1.0 / jnp.sum(scores, axis=-1, keepdims=True))
            mixed = jnp.dot(
                probs.astype(jnp.bfloat16), qkv[two, :, 256:], preferred_element_type=jnp.float32
            )
            mixed = jnp.where(lane < HD, mixed[:128], mixed[128:])
            out_ref[block, :, two * 128 : two * 128 + 128] = mixed.astype(jnp.bfloat16)
        return carry

    lax.fori_loop(0, 6, query_block, 0)


SMEM = pl.BlockSpec(memory_space=pltpu.SMEM)
VMEM = pl.BlockSpec(memory_space=pltpu.VMEM)
ANYWHERE = pl.BlockSpec(memory_space=pl.ANY)


def attend(place, length, temp, frames, weights):
    shard = frames[0].shape
    return pl.pallas_call(
        attend_kernel,
        out_shape=jax.ShapeDtypeStruct((6, shard[0], 256), jnp.bfloat16),
        in_specs=[SMEM] * 3 + [ANYWHERE] * 14 + [VMEM],
        out_specs=VMEM,
        scratch_shapes=[
            pltpu.VMEM((6,) + shard, jnp.bfloat16),
            pltpu.VMEM((8, 384, 384), jnp.bfloat16),
            pltpu.VMEM((2, 1536, 384), jnp.bfloat16),
            pltpu.VMEM((2, 6 * shard[0], 384), jnp.bfloat16),
            pltpu.SemaphoreType.DMA((14,)),
        ],
        compiler_params=pltpu.CompilerParams(vmem_limit_bytes=28 * 2**20),
        cost_estimate=pl.CostEstimate(
            flops=3 * 10**9, bytes_accessed=5 * 10**6, transcendentals=2 * 10**6
        ),
    )(place, length, temp, *frames, *weights, reorder())


def project_kernel(place_ref, heads_ref, *refs):
    own, other, move_ref, out_ref = refs[:4], refs[4:8], refs[8], refs[9]
    x, core = place_ref[1], place_ref[2]
    first = jnp.concatenate([heads_ref[at, :, :128] for at in range(6)], axis=1)
    second = jnp.concatenate([heads_ref[at, :, 128:] for at in range(6)], axis=1)
    mine = jnp.where(core == 0, first, second)
    given = jnp.where(core == 0, second, first)
    sides = (((1,), (1,)), ((), ()))
    for number, at in enumerate(x_places(x)):
        columns = pl.ds(pl.multiple_of(at * 384, 384), 384)
        total = lax.dot_general(
            mine, own[number][...], sides, preferred_element_type=jnp.float32
        ) + lax.dot_general(given, other[number][...], sides, preferred_element_type=jnp.float32)
        out_ref[:, columns] = jnp.dot(
            total.astype(jnp.bfloat16), move_ref[...], preferred_element_type=jnp.float32
        ).astype(jnp.bfloat16)


def project(place, heads, own, other):
    return pl.pallas_call(
        project_kernel,
        out_shape=jax.ShapeDtypeStruct((heads.shape[1], 1536), jnp.bfloat16),
        in_specs=[SMEM] + [VMEM] * 10,
        out_specs=VMEM,
        compiler_params=pltpu.CompilerParams(vmem_limit_bytes=20 * 2**20),
        cost_estimate=pl.CostEstimate(
            flops=8 * 10**8, bytes_accessed=6 * 10**6, transcendentals=0
        ),
    )(place, heads, *own, *other, reorder())


def on_device(latents, norm_gain, w_qkv, w_out, head_temp, lengths):
    frames = latents[0]
    values = frames.astype(jnp.float32)
    rms = jnp.sqrt(jnp.mean(values * values, axis=-1, keepdims=True) + 1e-06)
    normed = (values / rms * norm_gain).astype(jnp.bfloat16)
    across = other_triple(normed)

    rows = w_qkv.reshape(3, 12, 2, 128).transpose(2, 1, 0, 3).reshape(2, 12, 384)
    columns = w_out.T.reshape(12, 2, 128).transpose(1, 0, 2)
    both = jnp.concatenate([rows, columns], axis=2).reshape(1, 2, 48, 128)
    both = jnp.broadcast_to(both, (12, 2, 48, 128)).reshape(24, 48, 128)
    both = lax.all_to_all(after(both, normed), ("zh", "zl", "c"), 0, 0, tiled=True)
    both = both.reshape(2, 6, 2, 12, 512)
    rows = lax.dynamic_index_in_dim(both[..., :384], lax.axis_index("zl"), 1, keepdims=False)
    rows = rows.reshape(48, 384)
    columns = after(both, across)[..., 384:].transpose(0, 2, 3, 1, 4).reshape(48, 768)

    own_triple = [triple_shift(normed, 1), triple_shift(normed, 2)]
    by_y = gather_y(rows)
    out_by_y = gather_y(after(columns, by_y, *own_triple))
    by_x = gather_x(by_y)
    far_triple = [triple_shift(across, 1), triple_shift(across, 2)]
    other_by_x = [other_core(block) for block in by_x]
    out_own = gather_x(out_by_y)

    place = jnp.stack([lax.axis_index(axis) for axis in ("zl", "x", "c")]).astype(jnp.int32)
    blocks = attend(
        place,
        lengths,
        head_temp,
        [normed] + own_triple + [across] + far_triple,
        by_x + other_by_x,
    )
    own = lax.all_to_all(blocks, "zl", 0, 0, tiled=True)
    out_other = [other_core(block) for block in out_own]
    return project(place, own, out_own, out_other)[None]


def solution(mesh):
    split = Mesh(mesh.devices.reshape(SIZES), AXES)
    clip = ("x", "zh", "y", "c")
    in_specs = (
        P(clip, "zl", None),
        P(),
        P(None, clip, "zl"),
        P("zl", clip),
        P("zl"),
        P(clip),
    )
    out_specs = P(clip, "zl", None)
    return jax.shard_map(
        on_device, mesh=split, in_specs=in_specs, out_specs=out_specs, check_vma=False
    )
```

```python
import functools

import jax
import jax.numpy as jnp
import numpy as np
from jax import lax
from jax.experimental import pallas as pl
from jax.experimental.pallas import tpu as pltpu
from jax.sharding import Mesh, PartitionSpec as P

HD = 64
AXES = ("x", "zh", "y", "c", "zl")
SIZES = (4, 2, 8, 2, 6)


def permute(value, move):
    pairs = []
    for place in np.ndindex(*SIZES):
        goal = move(*place)
        if goal is not None:
            pairs.append(
                (int(np.ravel_multi_index(place, SIZES)), int(np.ravel_multi_index(goal, SIZES)))
            )
    return lax.ppermute(value, AXES, pairs)


def other_core(value):
    return permute(value, lambda x, zh, y, c, zl: (x, zh, y, 1 - c, zl))


def y_shift(value, step):
    return permute(value, lambda x, zh, y, c, zl: (x, zh, (y + step) % 8, c, zl))


def x_swap(value, which):
    goal = {"even": (1, 0, 3, 2), "odd": (3, 2, 1, 0), "across": (2, 3, 0, 1)}[which]
    return permute(value, lambda x, zh, y, c, zl: (goal[x], zh, y, c, zl))


def gather(value, axes, count):
    copies = jnp.broadcast_to(value[None], (count,) + value.shape)
    return lax.all_to_all(copies, axes, 0, 0, tiled=True).reshape(-1, value.shape[1])


def after(value, *others):
    return lax.optimization_barrier((value,) + others)[0]


def put(whole, block, at):
    return lax.dynamic_update_slice_in_dim(whole, block[None], at, 0)


def gather_x(block):
    x = lax.axis_index("x")
    whole = put(jnp.zeros((4,) + block.shape, block.dtype), block, x)
    for which, at in (("even", x ^ 1), ("odd", 3 - x), ("across", (x + 2) % 4)):
        whole = put(whole, x_swap(block, which), at)
    return whole.reshape(-1, block.shape[1])


def gather_y(block):
    y = lax.axis_index("y")
    whole = put(jnp.zeros((8,) + block.shape, block.dtype), block, y)
    up = down = block
    for step in range(1, 5):
        up = y_shift(up, 1)
        whole = put(whole, up, (y + 8 - step) % 8)
        if step < 4:
            down = y_shift(down, -1)
            whole = put(whole, down, (y + step) % 8)
    return whole.reshape(-1, block.shape[1])


def reorder():
    y, zh, r = np.meshgrid(np.arange(8), np.arange(2), np.arange(24), indexing="ij")
    matrix = np.zeros((384, 384), np.float32)
    matrix[np.arange(384), ((zh * 8 + y) * 24 + r).reshape(-1)] = 1
    return jnp.asarray(matrix, jnp.bfloat16)


def reorder_all():
    y, x, zh, r = np.meshgrid(
        np.arange(8), np.arange(4), np.arange(2), np.arange(24), indexing="ij"
    )
    matrix = np.zeros((1536, 1536), np.float32)
    matrix[np.arange(1536), (((x * 2 + zh) * 8 + y) * 24 + r).reshape(-1)] = 1
    return jnp.asarray(matrix, jnp.bfloat16)


def attend_kernel(core_ref, length_ref, temp_ref, frames, own_w, other_w, move_ref, *refs):
    out_ref, x_buf, w_in, w_buf, qkv, sems = refs
    core = core_ref[0]
    w_copies = [
        pltpu.make_async_copy(ref, w_in.at[number], sems.at[number])
        for number, ref in enumerate((own_w, other_w))
    ]
    x_copy = pltpu.make_async_copy(frames, x_buf, sems.at[2])
    for copy in w_copies + [x_copy]:
        copy.start()
    for which, half in ((0, core), (1, 1 - core)):
        w_copies[which].wait()
        for at in range(4):
            rows = slice(at * 384, at * 384 + 384)
            w_buf[half, rows, :] = lax.dot_general(
                move_ref[...],
                w_in[which, rows, :],
                (((0,), (0,)), ((), ())),
                preferred_element_type=jnp.float32,
            ).astype(jnp.bfloat16)
    x_copy.wait()

    total = x_buf.shape[0]
    for two in range(2):
        qkv[two] = jnp.dot(
            x_buf[...],
            w_buf[two],
            preferred_element_type=jnp.float32,
        ).astype(jnp.bfloat16)

    live = lax.broadcasted_iota(jnp.int32, (1, total), 1) < length_ref[0]
    lane = lax.broadcasted_iota(jnp.int32, (128, 128), 1)
    row = lax.broadcasted_iota(jnp.int32, (256, 1), 0)

    def query_block(block, carry):
        rows = pl.ds(pl.multiple_of(block * 128, 128), 128)
        for two in range(2):
            query = qkv[two, rows, :128]
            none = jnp.zeros_like(query)
            query = jnp.concatenate(
                [jnp.where(lane < HD, query, none), jnp.where(lane < HD, none, query)]
            )
            scores = lax.dot_general(
                query,
                qkv[two, :, 128:256],
                (((1,), (1,)), ((), ())),
                preferred_element_type=jnp.float32,
            )
            scale = jnp.where(row < 128, temp_ref[2 * two] / 8.0, temp_ref[2 * two + 1] / 8.0)
            scores = jnp.where(live, scores * scale, -1e30)
            scores = jnp.exp(scores - jnp.max(scores, axis=-1, keepdims=True))
            probs = scores * (1.0 / jnp.sum(scores, axis=-1, keepdims=True))
            mixed = jnp.dot(
                probs.astype(jnp.bfloat16), qkv[two, :, 256:], preferred_element_type=jnp.float32
            )
            mixed = jnp.where(lane < HD, mixed[:128], mixed[128:])
            out_ref[block, :, two * 128 : two * 128 + 128] = mixed.astype(jnp.bfloat16)
        return carry

    lax.fori_loop(0, 6, query_block, 0)


SMEM = pl.BlockSpec(memory_space=pltpu.SMEM)
VMEM = pl.BlockSpec(memory_space=pltpu.VMEM)
HBM = pl.BlockSpec(memory_space=pltpu.HBM)


def attend(core, length, temp, frames, own_w, other_w):
    rows, width = frames.shape
    return pl.pallas_call(
        attend_kernel,
        out_shape=jax.ShapeDtypeStruct((6, rows // 6, 256), jnp.bfloat16),
        in_specs=[SMEM] * 3 + [HBM] * 3 + [VMEM],
        out_specs=VMEM,
        scratch_shapes=[
            pltpu.VMEM((rows, width), jnp.bfloat16),
            pltpu.VMEM((2, width, 384), jnp.bfloat16),
            pltpu.VMEM((2, width, 384), jnp.bfloat16),
            pltpu.VMEM((2, rows, 384), jnp.bfloat16),
            pltpu.SemaphoreType.DMA((3,)),
        ],
        compiler_params=pltpu.CompilerParams(vmem_limit_bytes=58 * 2**20),
        cost_estimate=pl.CostEstimate(
            flops=3 * 10**9, bytes_accessed=5 * 10**6, transcendentals=2 * 10**6
        ),
    )(core, length, temp, frames, own_w, other_w, reorder())


def project_kernel(core_ref, heads_ref, own_ref, other_ref, move_hbm, out_ref, move_ref, sem):
    core = core_ref[0]
    move_copy = pltpu.make_async_copy(move_hbm, move_ref, sem)
    move_copy.start()
    first = jnp.concatenate([heads_ref[at, :, :128] for at in range(6)], axis=1)
    second = jnp.concatenate([heads_ref[at, :, 128:] for at in range(6)], axis=1)
    mine = jnp.where(core == 0, first, second)
    given = jnp.where(core == 0, second, first)
    sides = (((1,), (1,)), ((), ()))
    total = lax.dot_general(mine, own_ref[...], sides, preferred_element_type=jnp.float32)
    total += lax.dot_general(given, other_ref[...], sides, preferred_element_type=jnp.float32)
    move_copy.wait()
    out_ref[...] = jnp.dot(
        total.astype(jnp.bfloat16), move_ref[...], preferred_element_type=jnp.float32
    ).astype(jnp.bfloat16)


def project(core, heads, own, other):
    return pl.pallas_call(
        project_kernel,
        out_shape=jax.ShapeDtypeStruct((heads.shape[1], 1536), jnp.bfloat16),
        in_specs=[SMEM] + [VMEM] * 3 + [HBM],
        out_specs=VMEM,
        scratch_shapes=[pltpu.VMEM((1536, 1536), jnp.bfloat16), pltpu.SemaphoreType.DMA],
        compiler_params=pltpu.CompilerParams(vmem_limit_bytes=24 * 2**20),
        cost_estimate=pl.CostEstimate(
            flops=12 * 10**8, bytes_accessed=10 * 10**6, transcendentals=0
        ),
    )(core, heads, own, other, reorder_all())


def on_device(latents, norm_gain, w_qkv, w_out, head_temp, lengths):
    rows = w_qkv.reshape(3, 12, 2, 128).transpose(2, 1, 0, 3).reshape(2, 12, 384)
    columns = w_out.T.reshape(12, 2, 128).transpose(1, 0, 2)
    both = jnp.concatenate([rows, columns], axis=2).reshape(1, 2, 48, 128)
    both = jnp.broadcast_to(both, (12, 2, 48, 128)).reshape(24, 48, 128)
    both = lax.all_to_all(both, ("zh", "zl", "c"), 0, 0, tiled=True)
    both = both.reshape(2, 6, 2, 12, 512)
    rows = lax.dynamic_index_in_dim(both[..., :384], lax.axis_index("zl"), 1, keepdims=False)
    rows = rows.reshape(48, 384)

    frames = latents[0]
    values = frames.astype(jnp.float32)
    rms = jnp.sqrt(jnp.mean(values * values, axis=-1, keepdims=True) + 1e-06)
    normed = (values / rms * norm_gain).astype(jnp.bfloat16)
    whole = lax.all_gather(normed, "zl", axis=0, tiled=True)

    own_w = gather(rows, ("x", "y"), 32)
    other_w = other_core(own_w)
    columns = both[..., 384:].transpose(0, 2, 3, 1, 4).reshape(48, 768)
    out_own = gather_y(gather_x(columns))

    core = lax.axis_index("c").reshape(1).astype(jnp.int32)
    blocks = attend(core, lengths, head_temp, whole, own_w, other_w)
    own = lax.all_to_all(blocks, "zl", 0, 0, tiled=True)
    out_other = other_core(out_own)
    return project(core, own, out_own, out_other)[None]


def solution(mesh):
    split = Mesh(mesh.devices.reshape(SIZES), AXES)
    clip = ("x", "zh", "y", "c")
    in_specs = (
        P(clip, "zl", None),
        P(),
        P(None, clip, "zl"),
        P("zl", clip),
        P("zl"),
        P(clip),
    )
    out_specs = P(clip, "zl", None)
    return jax.shard_map(
        on_device, mesh=split, in_specs=in_specs, out_specs=out_specs, check_vma=False
    )
```

```python
import functools

import jax
import jax.numpy as jnp
import numpy as np
from jax import lax
from jax.experimental import pallas as pl
from jax.experimental.pallas import tpu as pltpu
from jax.sharding import Mesh, PartitionSpec as P

HD = 64
AXES = ("x", "zh", "y", "c", "zl")
SIZES = (4, 2, 8, 2, 6)


def permute(value, move):
    pairs = []
    for place in np.ndindex(*SIZES):
        goal = move(*place)
        if goal is not None:
            pairs.append(
                (int(np.ravel_multi_index(place, SIZES)), int(np.ravel_multi_index(goal, SIZES)))
            )
    return lax.ppermute(value, AXES, pairs)


def other_core(value):
    return permute(value, lambda x, zh, y, c, zl: (x, zh, y, 1 - c, zl))


def other_triple(value):
    return permute(value, lambda x, zh, y, c, zl: (x, zh, y, c, (zl + 3) % 6))


def triple_shift(value, step):
    return permute(
        value, lambda x, zh, y, c, zl: (x, zh, y, c, zl // 3 * 3 + (zl + step) % 3)
    )


def y_shift(value, step):
    return permute(value, lambda x, zh, y, c, zl: (x, zh, (y + step) % 8, c, zl))


def x_swap(value, which):
    goal = {"even": (1, 0, 3, 2), "odd": (3, 2, 1, 0), "across": (2, 3, 0, 1)}[which]
    return permute(value, lambda x, zh, y, c, zl: (goal[x], zh, y, c, zl))


def gather(value, axes, count):
    copies = jnp.broadcast_to(value[None], (count,) + value.shape)
    return lax.all_to_all(copies, axes, 0, 0, tiled=True).reshape(-1, value.shape[1])


def after(value, *others):
    return lax.optimization_barrier((value,) + others)[0]


def put(whole, block, at):
    return lax.dynamic_update_slice_in_dim(whole, block[None], at, 0)


def gather_x(block, tie):
    x = lax.axis_index("x")
    whole = put(jnp.zeros((4,) + block.shape, block.dtype), block, x)
    whole = put(whole, x_swap(block, "even"), x ^ 1)
    whole = put(whole, x_swap(block, "odd"), 3 - x)
    whole = put(whole, x_swap(after(block, *tie), "across"), (x + 2) % 4)
    return whole.reshape(-1, block.shape[1])


def ring_y(block):
    ups, downs = [block], [block]
    for step in range(1, 5):
        ups.append(y_shift(ups[-1], 1))
        if step < 4:
            downs.append(y_shift(downs[-1], -1))
    return ups, downs


def reorder():
    y, zh, r = np.meshgrid(np.arange(8), np.arange(2), np.arange(24), indexing="ij")
    matrix = np.zeros((384, 384), np.float32)
    matrix[np.arange(384), ((zh * 8 + y) * 24 + r).reshape(-1)] = 1
    return jnp.asarray(matrix, jnp.bfloat16)


def reorder_all():
    y, x, zh, r = np.meshgrid(
        np.arange(8), np.arange(4), np.arange(2), np.arange(24), indexing="ij"
    )
    matrix = np.zeros((1536, 1536), np.float32)
    matrix[np.arange(1536), (((x * 2 + zh) * 8 + y) * 24 + r).reshape(-1)] = 1
    return jnp.asarray(matrix, jnp.bfloat16)


def attend_kernel(place_ref, length_ref, temp_ref, *refs):
    frames, weights, move_ref, out_ref = refs[:6], refs[6:8], refs[8], refs[9]
    x_buf, w_in, w_buf, qkv, sems = refs[10:]
    place, core = place_ref[0], place_ref[1]
    base, within = place // 3 * 3, lax.rem(place, 3)
    below, above = lax.rem(within + 2, 3), lax.rem(within + 1, 3)
    slots = (
        place,
        base + below,
        base + above,
        3 - base + within,
        3 - base + below,
        3 - base + above,
    )
    w_copies = [
        pltpu.make_async_copy(ref, w_in.at[number], sems.at[6 + number])
        for number, ref in enumerate(weights)
    ]
    copies = [
        pltpu.make_async_copy(ref, x_buf.at[at], sems.at[number])
        for number, (ref, at) in enumerate(zip(frames, slots))
    ]
    for copy in w_copies + copies:
        copy.start()
    for which, half in ((0, core), (1, 1 - core)):
        w_copies[which].wait()
        for at in range(4):
            rows = slice(at * 384, at * 384 + 384)
            w_buf[half, rows, :] = lax.dot_general(
                move_ref[...],
                w_in[which, rows, :],
                (((0,), (0,)), ((), ())),
                preferred_element_type=jnp.float32,
            ).astype(jnp.bfloat16)
    for copy in copies:
        copy.wait()

    total = x_buf.shape[0] * x_buf.shape[1]
    for two in range(2):
        qkv[two] = jnp.dot(
            x_buf[...].reshape(total, x_buf.shape[2]),
            w_buf[two],
            preferred_element_type=jnp.float32,
        ).astype(jnp.bfloat16)

    live = lax.broadcasted_iota(jnp.int32, (1, total), 1) < length_ref[0]
    lane = lax.broadcasted_iota(jnp.int32, (128, 128), 1)
    row = lax.broadcasted_iota(jnp.int32, (256, 1), 0)

    def query_block(block, carry):
        rows = pl.ds(pl.multiple_of(block * 128, 128), 128)
        for two in range(2):
            query = qkv[two, rows, :128]
            none = jnp.zeros_like(query)
            query = jnp.concatenate(
                [jnp.where(lane < HD, query, none), jnp.where(lane < HD, none, query)]
            )
            scores = lax.dot_general(
                query,
                qkv[two, :, 128:256],
                (((1,), (1,)), ((), ())),
                preferred_element_type=jnp.float32,
            )
            scale = jnp.where(row < 128, temp_ref[2 * two] / 8.0, temp_ref[2 * two + 1] / 8.0)
            scores = jnp.where(live, scores * scale, -1e30)
            scores = jnp.exp(scores - jnp.max(scores, axis=-1, keepdims=True))
            probs = scores * (1.0 / jnp.sum(scores, axis=-1, keepdims=True))
            mixed = jnp.dot(
                probs.astype(jnp.bfloat16), qkv[two, :, 256:], preferred_element_type=jnp.float32
            )
            mixed = jnp.where(lane < HD, mixed[:128], mixed[128:])
            out_ref[block, :, two * 128 : two * 128 + 128] = mixed.astype(jnp.bfloat16)
        return carry

    lax.fori_loop(0, 6, query_block, 0)


SMEM = pl.BlockSpec(memory_space=pltpu.SMEM)
VMEM = pl.BlockSpec(memory_space=pltpu.VMEM)
HBM = pl.BlockSpec(memory_space=pltpu.HBM)


def attend(place, length, temp, frames, weights):
    shard = frames[0].shape
    return pl.pallas_call(
        attend_kernel,
        out_shape=jax.ShapeDtypeStruct((6, shard[0], 256), jnp.bfloat16),
        in_specs=[SMEM] * 3 + [HBM] * 8 + [VMEM],
        out_specs=VMEM,
        scratch_shapes=[
            pltpu.VMEM((6,) + shard, jnp.bfloat16),
            pltpu.VMEM((2, 1536, 384), jnp.bfloat16),
            pltpu.VMEM((2, 1536, 384), jnp.bfloat16),
            pltpu.VMEM((2, 6 * shard[0], 384), jnp.bfloat16),
            pltpu.SemaphoreType.DMA((8,)),
        ],
        compiler_params=pltpu.CompilerParams(vmem_limit_bytes=58 * 2**20),
        cost_estimate=pl.CostEstimate(
            flops=3 * 10**9, bytes_accessed=5 * 10**6, transcendentals=2 * 10**6
        ),
    )(place, length, temp, *frames, *weights, reorder())


def project_kernel(place_ref, heads_ref, *refs):
    own, other = refs[:8], (refs[8], refs[9])
    move_hbm, out_ref, parts, move_ref, sem = refs[10:]
    core, y = place_ref[1], place_ref[2]
    move_copy = pltpu.make_async_copy(move_hbm, move_ref, sem)
    move_copy.start()
    first = jnp.concatenate([heads_ref[at, :, :128] for at in range(6)], axis=1)
    second = jnp.concatenate([heads_ref[at, :, 128:] for at in range(6)], axis=1)
    mine = jnp.where(core == 0, first, second)
    given = jnp.where(core == 0, second, first)
    sides = (((1,), (1,)), ((), ()))
    for number, distance in enumerate((0, 7, 1, 6, 2, 5, 3, 4)):
        part = lax.dot_general(mine, own[number][...], sides, preferred_element_type=jnp.float32)
        rows = other[0][number] if number < 5 else other[1][number - 5]
        part += lax.dot_general(given, rows, sides, preferred_element_type=jnp.float32)
        parts[lax.rem(y + distance, 8)] = part.astype(jnp.bfloat16)
    move_copy.wait()
    total = jnp.zeros(out_ref.shape, jnp.float32)
    for at in range(8):
        total += jnp.dot(
            parts[at], move_ref[at * 192 : at * 192 + 192], preferred_element_type=jnp.float32
        )
    out_ref[...] = total.astype(jnp.bfloat16)


def project(place, heads, own, other):
    rows = heads.shape[1]
    return pl.pallas_call(
        project_kernel,
        out_shape=jax.ShapeDtypeStruct((rows, 1536), jnp.bfloat16),
        in_specs=[SMEM] + [VMEM] * 11 + [HBM],
        out_specs=VMEM,
        scratch_shapes=[
            pltpu.VMEM((8, rows, 192), jnp.bfloat16),
            pltpu.VMEM((1536, 1536), jnp.bfloat16),
            pltpu.SemaphoreType.DMA,
        ],
        compiler_params=pltpu.CompilerParams(vmem_limit_bytes=24 * 2**20),
        cost_estimate=pl.CostEstimate(
            flops=12 * 10**8, bytes_accessed=10 * 10**6, transcendentals=0
        ),
    )(place, heads, *own, *other, reorder_all())


def on_device(latents, norm_gain, w_qkv, w_out, head_temp, lengths):
    rows = w_qkv.reshape(3, 12, 2, 128).transpose(2, 1, 0, 3).reshape(2, 12, 384)
    columns = w_out.T.reshape(12, 2, 128).transpose(1, 0, 2)
    both = jnp.concatenate([rows, columns], axis=2).reshape(1, 2, 48, 128)
    both = jnp.broadcast_to(both, (12, 2, 48, 128)).reshape(24, 48, 128)
    both = lax.all_to_all(both, ("zh", "zl", "c"), 0, 0, tiled=True)
    both = both.reshape(2, 6, 2, 12, 512)
    rows = lax.dynamic_index_in_dim(both[..., :384], lax.axis_index("zl"), 1, keepdims=False)
    rows = rows.reshape(48, 384)

    frames = latents[0]
    values = frames.astype(jnp.float32)
    rms = jnp.sqrt(jnp.mean(values * values, axis=-1, keepdims=True) + 1e-06)
    normed = (values / rms * norm_gain).astype(jnp.bfloat16)
    across = other_triple(normed)
    own_triple = [triple_shift(normed, 1), triple_shift(normed, 2)]
    far_triple = [triple_shift(across, 1), triple_shift(across, 2)]

    columns = both[..., 384:].transpose(0, 2, 3, 1, 4).reshape(48, 768)

    by_y = gather(after(rows, normed), "y", 8)
    out_by_x = gather_x(columns, [across])
    own_w = gather(by_y, "x", 4)
    other_w = other_core(own_w)
    ups, downs = ring_y(after(out_by_x, *own_triple))
    out_own = [ups[0], ups[1], downs[1], ups[2], downs[2], ups[3], downs[3], ups[4]]
    out_other = [other_core(jnp.stack(out_own[:5])), other_core(jnp.stack(out_own[5:]))]

    place = jnp.stack([lax.axis_index(axis) for axis in ("zl", "c", "y")]).astype(jnp.int32)
    blocks = attend(
        place,
        lengths,
        head_temp,
        [normed] + own_triple + [across] + far_triple,
        [own_w, other_w],
    )
    own = lax.all_to_all(blocks, "zl", 0, 0, tiled=True)
    return project(place, own, out_own, out_other)[None]


def solution(mesh):
    split = Mesh(mesh.devices.reshape(SIZES), AXES)
    clip = ("x", "zh", "y", "c")
    in_specs = (
        P(clip, "zl", None),
        P(),
        P(None, clip, "zl"),
        P("zl", clip),
        P("zl"),
        P(clip),
    )
    out_specs = P(clip, "zl", None)
    return jax.shard_map(
        on_device, mesh=split, in_specs=in_specs, out_specs=out_specs, check_vma=False
    )
```

```python
import functools

import jax
import jax.numpy as jnp
import numpy as np
from jax import lax
from jax.experimental import pallas as pl
from jax.experimental.pallas import tpu as pltpu
from jax.sharding import Mesh, PartitionSpec as P

HD = 64
AXES = ("x", "zh", "y", "c", "zl")
SIZES = (4, 2, 8, 2, 6)


def permute(value, move):
    pairs = []
    for place in np.ndindex(*SIZES):
        goal = move(*place)
        if goal is not None:
            pairs.append(
                (int(np.ravel_multi_index(place, SIZES)), int(np.ravel_multi_index(goal, SIZES)))
            )
    return lax.ppermute(value, AXES, pairs)


def other_core(value):
    return permute(value, lambda x, zh, y, c, zl: (x, zh, y, 1 - c, zl))


def x_swap(value, which):
    goal = {"even": (1, 0, 3, 2), "odd": (3, 2, 1, 0), "across": (2, 3, 0, 1)}[which]
    return permute(value, lambda x, zh, y, c, zl: (goal[x], zh, y, c, zl))


def gather(value, axes, count):
    copies = jnp.broadcast_to(value[None], (count,) + value.shape)
    return lax.all_to_all(copies, axes, 0, 0, tiled=True).reshape(-1, value.shape[1])


def after(value, *others):
    return lax.optimization_barrier((value,) + others)[0]


def gather_x(block):
    x = lax.axis_index("x")
    whole = jnp.zeros((4,) + block.shape, block.dtype)
    for value, at in (
        (block, x),
        (x_swap(block, "even"), x ^ 1),
        (x_swap(block, "odd"), 3 - x),
        (x_swap(block, "across"), (x + 2) % 4),
    ):
        whole = lax.dynamic_update_slice_in_dim(whole, value[None], at, 0)
    return whole.reshape(-1, block.shape[1])


def reorder():
    y, zh, r = np.meshgrid(np.arange(8), np.arange(2), np.arange(24), indexing="ij")
    matrix = np.zeros((384, 384), np.float32)
    matrix[np.arange(384), ((zh * 8 + y) * 24 + r).reshape(-1)] = 1
    return jnp.asarray(matrix, jnp.bfloat16)


def reorder_all():
    y, x, zh, r = np.meshgrid(
        np.arange(8), np.arange(4), np.arange(2), np.arange(24), indexing="ij"
    )
    matrix = np.zeros((1536, 1536), np.float32)
    matrix[np.arange(1536), (((x * 2 + zh) * 8 + y) * 24 + r).reshape(-1)] = 1
    return jnp.asarray(matrix, jnp.bfloat16)


def attend_kernel(core_ref, length_ref, temp_ref, frames, own_w, other_w, move_ref, *refs):
    out_ref, x_buf, w_in, w_buf, qkv, sems = refs
    core = core_ref[0]
    w_copies = [
        pltpu.make_async_copy(ref, w_in.at[number], sems.at[number])
        for number, ref in enumerate((own_w, other_w))
    ]
    x_copy = pltpu.make_async_copy(frames, x_buf, sems.at[2])
    for copy in w_copies + [x_copy]:
        copy.start()
    for which, half in ((0, core), (1, 1 - core)):
        w_copies[which].wait()
        for number in range(4):
            rows = slice(number * 384, number * 384 + 384)
            w_buf[half, rows, :] = lax.dot_general(
                move_ref[...],
                w_in[which, number],
                (((0,), (0,)), ((), ())),
                preferred_element_type=jnp.float32,
            ).astype(jnp.bfloat16)
    x_copy.wait()

    total = x_buf.shape[0]
    for two in range(2):
        qkv[two] = jnp.dot(
            x_buf[...],
            w_buf[two],
            preferred_element_type=jnp.float32,
        ).astype(jnp.bfloat16)

    live = lax.broadcasted_iota(jnp.int32, (1, total), 1) < length_ref[0]
    lane = lax.broadcasted_iota(jnp.int32, (128, 128), 1)
    row = lax.broadcasted_iota(jnp.int32, (256, 1), 0)

    def query_block(block, carry):
        rows = pl.ds(pl.multiple_of(block * 128, 128), 128)
        for two in range(2):
            query = qkv[two, rows, :128]
            none = jnp.zeros_like(query)
            query = jnp.concatenate(
                [jnp.where(lane < HD, query, none), jnp.where(lane < HD, none, query)]
            )
            scores = lax.dot_general(
                query,
                qkv[two, :, 128:256],
                (((1,), (1,)), ((), ())),
                preferred_element_type=jnp.float32,
            )
            scale = jnp.where(row < 128, temp_ref[2 * two] / 8.0, temp_ref[2 * two + 1] / 8.0)
            scores = jnp.where(live, scores * scale, -1e30)
            scores = jnp.exp(scores - jnp.max(scores, axis=-1, keepdims=True))
            probs = scores * (1.0 / jnp.sum(scores, axis=-1, keepdims=True))
            mixed = jnp.dot(
                probs.astype(jnp.bfloat16), qkv[two, :, 256:], preferred_element_type=jnp.float32
            )
            mixed = jnp.where(lane < HD, mixed[:128], mixed[128:])
            out_ref[block, :, two * 128 : two * 128 + 128] = mixed.astype(jnp.bfloat16)
        return carry

    lax.fori_loop(0, 6, query_block, 0)


SMEM = pl.BlockSpec(memory_space=pltpu.SMEM)
VMEM = pl.BlockSpec(memory_space=pltpu.VMEM)
HBM = pl.BlockSpec(memory_space=pltpu.HBM)


def attend(core, length, temp, frames, own_w, other_w):
    rows, width = frames.shape
    return pl.pallas_call(
        attend_kernel,
        out_shape=jax.ShapeDtypeStruct((6, rows // 6, 256), jnp.bfloat16),
        in_specs=[SMEM] * 3 + [HBM] * 3 + [VMEM],
        out_specs=VMEM,
        scratch_shapes=[
            pltpu.VMEM((rows, width), jnp.bfloat16),
            pltpu.VMEM((2, 4, 384, 384), jnp.bfloat16),
            pltpu.VMEM((2, width, 384), jnp.bfloat16),
            pltpu.VMEM((2, rows, 384), jnp.bfloat16),
            pltpu.SemaphoreType.DMA((3,)),
        ],
        compiler_params=pltpu.CompilerParams(vmem_limit_bytes=58 * 2**20),
        cost_estimate=pl.CostEstimate(
            flops=3 * 10**9, bytes_accessed=5 * 10**6, transcendentals=2 * 10**6
        ),
    )(core, length, temp, frames, own_w, other_w, reorder())


def project_kernel(core_ref, heads_hbm, own_hbm, other_hbm, move_hbm, out_ref, *scratch):
    heads_ref, own_ref, other_ref, move_ref, sems = scratch
    core = core_ref[0]
    copies = [
        pltpu.make_async_copy(source, goal, sems.at[number])
        for number, (source, goal) in enumerate(
            (
                (heads_hbm, heads_ref),
                (own_hbm, own_ref),
                (other_hbm, other_ref),
                (move_hbm, move_ref),
            )
        )
    ]
    for copy in copies:
        copy.start()
    copies[0].wait()
    first = jnp.concatenate([heads_ref[at, :, :128] for at in range(6)], axis=1)
    second = jnp.concatenate([heads_ref[at, :, 128:] for at in range(6)], axis=1)
    mine = jnp.where(core == 0, first, second)
    given = jnp.where(core == 0, second, first)
    sides = (((1,), (1,)), ((), ()))
    copies[1].wait()
    total = lax.dot_general(mine, own_ref[...], sides, preferred_element_type=jnp.float32)
    copies[2].wait()
    total += lax.dot_general(given, other_ref[...], sides, preferred_element_type=jnp.float32)
    copies[3].wait()
    out_ref[...] = jnp.dot(
        total.astype(jnp.bfloat16), move_ref[...], preferred_element_type=jnp.float32
    ).astype(jnp.bfloat16)


def project(core, heads, own, other):
    return pl.pallas_call(
        project_kernel,
        out_shape=jax.ShapeDtypeStruct((heads.shape[1], 1536), jnp.bfloat16),
        in_specs=[SMEM] + [HBM] * 4,
        out_specs=VMEM,
        scratch_shapes=[
            pltpu.VMEM(heads.shape, jnp.bfloat16),
            pltpu.VMEM(own.shape, jnp.bfloat16),
            pltpu.VMEM(own.shape, jnp.bfloat16),
            pltpu.VMEM((1536, 1536), jnp.bfloat16),
            pltpu.SemaphoreType.DMA((4,)),
        ],
        compiler_params=pltpu.CompilerParams(vmem_limit_bytes=58 * 2**20),
        cost_estimate=pl.CostEstimate(
            flops=12 * 10**8, bytes_accessed=10 * 10**6, transcendentals=0
        ),
    )(core, heads, own, other, reorder_all())


def on_device(latents, norm_gain, w_qkv, w_out, head_temp, lengths):
    frames = latents[0]
    values = frames.astype(jnp.float32)
    rms = jnp.sqrt(jnp.mean(values * values, axis=-1, keepdims=True) + 1e-06)
    normed = (values / rms * norm_gain).astype(jnp.bfloat16)
    whole = lax.all_gather(normed, "zl", axis=0, tiled=True)

    rows = w_qkv.reshape(3, 12, 2, 128).transpose(2, 1, 0, 3).reshape(2, 12, 384)
    columns = w_out.T.reshape(12, 2, 128).transpose(1, 0, 2)
    both = jnp.concatenate([rows, columns], axis=2).reshape(1, 2, 48, 128)
    both = jnp.broadcast_to(both, (12, 2, 48, 128)).reshape(24, 48, 128)
    both = lax.all_to_all(after(both, normed), ("zh", "zl", "c"), 0, 0, tiled=True)
    both = both.reshape(2, 6, 2, 12, 512)
    rows = lax.dynamic_index_in_dim(both[..., :384], lax.axis_index("zl"), 1, keepdims=False)
    rows = rows.reshape(48, 384)
    by_y = gather(rows, "y", 8)
    columns = both[..., 384:].transpose(0, 2, 3, 1, 4).reshape(48, 768)
    own_w = gather(by_y, "x", 4).reshape(4, 384, 384)
    out_by_x, own_w = lax.optimization_barrier((gather_x(columns), own_w))
    other_w = other_core(own_w)
    out_own = lax.all_gather(out_by_x, "y", axis=0, tiled=True)

    core = lax.axis_index("c").reshape(1).astype(jnp.int32)
    blocks = attend(core, lengths, head_temp, whole, own_w, other_w)
    own = lax.all_to_all(blocks, "zl", 0, 0, tiled=True)
    own, out_own = lax.optimization_barrier((own, out_own))
    out_other = other_core(out_own)
    return project(core, own, out_own, out_other)[None]


def solution(mesh):
    split = Mesh(mesh.devices.reshape(SIZES), AXES)
    clip = ("x", "zh", "y", "c")
    in_specs = (
        P(clip, "zl", None),
        P(),
        P(None, clip, "zl"),
        P("zl", clip),
        P("zl"),
        P(clip),
    )
    out_specs = P(clip, "zl", None)
    return jax.shard_map(
        on_device, mesh=split, in_specs=in_specs, out_specs=out_specs, check_vma=False
    )
```

```python
import functools

import jax
import jax.numpy as jnp
import numpy as np
from jax import lax
from jax.experimental import pallas as pl
from jax.experimental.pallas import tpu as pltpu
from jax.sharding import Mesh, PartitionSpec as P

HD = 64
AXES = ("x", "zh", "y", "c", "zl")
SIZES = (4, 2, 8, 2, 6)


def permute(value, move):
    pairs = []
    for place in np.ndindex(*SIZES):
        goal = move(*place)
        if goal is not None:
            pairs.append(
                (int(np.ravel_multi_index(place, SIZES)), int(np.ravel_multi_index(goal, SIZES)))
            )
    return lax.ppermute(value, AXES, pairs)


def other_core(value):
    return permute(value, lambda x, zh, y, c, zl: (x, zh, y, 1 - c, zl))


def x_swap(value, which):
    goal = {"even": (1, 0, 3, 2), "odd": (3, 2, 1, 0), "across": (2, 3, 0, 1)}[which]
    return permute(value, lambda x, zh, y, c, zl: (goal[x], zh, y, c, zl))


def gather(value, axes, count):
    copies = jnp.broadcast_to(value[None], (count,) + value.shape)
    return lax.all_to_all(copies, axes, 0, 0, tiled=True).reshape(-1, value.shape[1])


def after(value, *others):
    return lax.optimization_barrier((value,) + others)[0]


def gather_x(block):
    x = lax.axis_index("x")
    whole = jnp.zeros((4,) + block.shape, block.dtype)
    for value, at in (
        (block, x),
        (x_swap(block, "even"), x ^ 1),
        (x_swap(block, "odd"), 3 - x),
        (x_swap(block, "across"), (x + 2) % 4),
    ):
        whole = lax.dynamic_update_slice_in_dim(whole, value[None], at, 0)
    return whole.reshape(-1, block.shape[1])


def attend_kernel(core_ref, length_ref, temp_ref, frames, own_w, other_w, *refs):
    out_ref, x_buf, w_buf, qkv, sems = refs
    core = core_ref[0]
    copies = []
    for number in range(4):
        rows = pl.ds(number * 384, 384)
        for source, half in ((own_w, core), (other_w, 1 - core)):
            columns = pl.ds(pl.multiple_of(half * 384, 128), 384)
            copies.append((source.at[rows], w_buf.at[rows, columns]))
    for number in range(6):
        rows = pl.ds(number * 128, 128)
        copies.append((frames.at[rows], x_buf.at[rows]))
    copies = [
        pltpu.make_async_copy(source, goal, sems.at[number])
        for number, (source, goal) in enumerate(copies)
    ]
    for copy in copies:
        copy.start()
    for copy in copies:
        copy.wait()
    qkv[...] = jnp.dot(
        x_buf[...], w_buf[...], preferred_element_type=jnp.float32
    ).astype(jnp.bfloat16)

    total = x_buf.shape[0]
    live = lax.broadcasted_iota(jnp.int32, (total, 1), 0) < length_ref[0]
    lane = lax.broadcasted_iota(jnp.int32, (total, 128), 1)
    place = lax.broadcasted_iota(jnp.int32, (1, 2 * total), 1)
    for two in range(2):
        query, key_part, value = (
            qkv[:, two * 384 + k * 128 : two * 384 + k * 128 + 128] for k in range(3)
        )
        none = jnp.zeros_like(query)
        query = jnp.concatenate(
            [jnp.where(lane < HD, query, none), jnp.where(lane < HD, none, query)]
        )
        scores = lax.dot_general(
            key_part, query, (((1,), (1,)), ((), ())), preferred_element_type=jnp.float32
        )
        scale = jnp.where(place < total, temp_ref[2 * two] / 8.0, temp_ref[2 * two + 1] / 8.0)
        scores = jnp.where(live, scores * scale, -1e30)
        scores = jnp.exp(scores - jnp.max(scores, axis=0, keepdims=True))
        mixed = lax.dot_general(
            value,
            scores.astype(jnp.bfloat16),
            (((0,), (0,)), ((), ())),
            preferred_element_type=jnp.float32,
        )
        mixed = mixed / jnp.sum(scores, axis=0, keepdims=True)
        mixed = jnp.concatenate([mixed[:HD, :total], mixed[HD:, total:]]).T
        out_ref[:, :, two * 128 : two * 128 + 128] = mixed.astype(jnp.bfloat16).reshape(
            out_ref.shape[0], out_ref.shape[1], 128
        )


SMEM = pl.BlockSpec(memory_space=pltpu.SMEM)
VMEM = pl.BlockSpec(memory_space=pltpu.VMEM)
ANYWHERE = pl.BlockSpec(memory_space=pl.ANY)


def attend(core, length, temp, frames, own_w, other_w):
    rows, width = frames.shape
    return pl.pallas_call(
        attend_kernel,
        out_shape=jax.ShapeDtypeStruct((6, rows // 6, 256), jnp.bfloat16),
        in_specs=[SMEM] * 3 + [ANYWHERE] * 3,
        out_specs=VMEM,
        scratch_shapes=[
            pltpu.VMEM((rows, width), jnp.bfloat16),
            pltpu.VMEM((width, 768), jnp.bfloat16),
            pltpu.VMEM((rows, 768), jnp.bfloat16),
            pltpu.SemaphoreType.DMA((14,)),
        ],
        compiler_params=pltpu.CompilerParams(vmem_limit_bytes=58 * 2**20),
        cost_estimate=pl.CostEstimate(
            flops=3 * 10**9, bytes_accessed=5 * 10**6, transcendentals=2 * 10**6
        ),
    )(core, length, temp, frames, own_w, other_w)


def project_kernel(core_ref, heads_any, own_any, other_any, out_ref, *scratch):
    heads_ref, own_ref, other_ref, sums, sems = scratch
    core = core_ref[0]
    copies = [(heads_any, heads_ref)]
    for source, goal in ((own_any, own_ref), (other_any, other_ref)):
        for number in range(4):
            rows = pl.ds(number * 384, 384)
            copies.append((source.at[rows], goal.at[rows]))
    copies = [
        pltpu.make_async_copy(source, goal, sems.at[number])
        for number, (source, goal) in enumerate(copies)
    ]
    for copy in copies:
        copy.start()
    copies[0].wait()
    first = jnp.concatenate([heads_ref[at, :, :128] for at in range(6)], axis=1)
    second = jnp.concatenate([heads_ref[at, :, 128:] for at in range(6)], axis=1)
    mine = jnp.where(core == 0, first, second).T
    given = jnp.where(core == 0, second, first).T
    for number in range(4):
        rows = pl.ds(number * 384, 384)
        copies[1 + number].wait()
        sums[rows] = jnp.dot(own_ref[rows], mine, preferred_element_type=jnp.float32)
    for number in range(4):
        rows = pl.ds(number * 384, 384)
        copies[5 + number].wait()
        sums[rows] += jnp.dot(other_ref[rows], given, preferred_element_type=jnp.float32)
    for x in range(4):
        pieces = []
        for zh in range(2):
            for y in range(8):
                at = ((y * 4 + x) * 2 + zh) * 24
                pieces.append(sums[at : at + 24, :])
        block = jnp.concatenate(pieces).T
        out_ref[:, x * 384 : x * 384 + 384] = block.astype(jnp.bfloat16)


def project(core, heads, own, other):
    rows = heads.shape[1]
    return pl.pallas_call(
        project_kernel,
        out_shape=jax.ShapeDtypeStruct((rows, 1536), jnp.bfloat16),
        in_specs=[SMEM] + [ANYWHERE] * 3,
        out_specs=VMEM,
        scratch_shapes=[
            pltpu.VMEM(heads.shape, jnp.bfloat16),
            pltpu.VMEM(own.shape, jnp.bfloat16),
            pltpu.VMEM(own.shape, jnp.bfloat16),
            pltpu.VMEM((1536, rows), jnp.float32),
            pltpu.SemaphoreType.DMA((9,)),
        ],
        compiler_params=pltpu.CompilerParams(vmem_limit_bytes=58 * 2**20),
        cost_estimate=pl.CostEstimate(
            flops=6 * 10**8, bytes_accessed=5 * 10**6, transcendentals=0
        ),
    )(core, heads, own, other)


def on_device(latents, norm_gain, w_qkv, w_out, head_temp, lengths):
    frames = latents[0]
    values = frames.astype(jnp.float32)
    rms = jnp.sqrt(jnp.mean(values * values, axis=-1, keepdims=True) + 1e-06)
    normed = (values / rms * norm_gain).astype(jnp.bfloat16)
    whole = lax.all_gather(normed, "zl", axis=0, tiled=True)

    rows = w_qkv.reshape(3, 12, 2, 128).transpose(2, 1, 0, 3).reshape(2, 12, 384)
    columns = w_out.T.reshape(12, 2, 128).transpose(1, 0, 2)
    both = jnp.concatenate([rows, columns], axis=2).reshape(1, 2, 48, 128)
    both = jnp.broadcast_to(both, (12, 2, 48, 128)).reshape(24, 48, 128)
    both = lax.all_to_all(after(both, normed), ("zh", "zl", "c"), 0, 0, tiled=True)
    both = both.reshape(2, 6, 2, 12, 512)
    rows = lax.dynamic_index_in_dim(both[..., :384], lax.axis_index("zl"), 1, keepdims=False)
    rows = rows.reshape(48, 384)
    by_y = gather(rows, "y", 8).reshape(8, 2, 24, 384).transpose(1, 0, 2, 3).reshape(384, 384)
    columns = both[..., 384:].transpose(0, 2, 3, 1, 4).reshape(48, 768)
    own_w = gather(by_y, "x", 4)
    out_by_x, own_w = lax.optimization_barrier((gather_x(columns), own_w))
    other_w = other_core(own_w)
    out_own = lax.all_gather(out_by_x, "y", axis=0, tiled=True)

    core = lax.axis_index("c").reshape(1).astype(jnp.int32)
    blocks = attend(core, lengths, head_temp, whole, own_w, other_w)
    own = lax.all_to_all(blocks, "zl", 0, 0, tiled=True)
    own, out_own = lax.optimization_barrier((own, out_own))
    out_other = other_core(out_own)
    return project(core, own, out_own, out_other)[None]


def solution(mesh):
    split = Mesh(mesh.devices.reshape(SIZES), AXES)
    clip = ("x", "zh", "y", "c")
    in_specs = (
        P(clip, "zl", None),
        P(),
        P(None, clip, "zl"),
        P("zl", clip),
        P("zl"),
        P(clip),
    )
    out_specs = P(clip, "zl", None)
    return jax.shard_map(
        on_device, mesh=split, in_specs=in_specs, out_specs=out_specs, check_vma=False
    )
```

```python
import functools

import jax
import jax.numpy as jnp
import numpy as np
from jax import lax
from jax.experimental import pallas as pl
from jax.experimental.pallas import tpu as pltpu
from jax.sharding import Mesh, PartitionSpec as P

HD = 64
AXES = ("x", "zh", "y", "c", "zl")
SIZES = (4, 2, 8, 2, 6)


def permute(value, move):
    pairs = []
    for place in np.ndindex(*SIZES):
        goal = move(*place)
        if goal is not None:
            pairs.append(
                (int(np.ravel_multi_index(place, SIZES)), int(np.ravel_multi_index(goal, SIZES)))
            )
    return lax.ppermute(value, AXES, pairs)


def other_core(value):
    return permute(value, lambda x, zh, y, c, zl: (x, zh, y, 1 - c, zl))


def other_triple(value):
    return permute(value, lambda x, zh, y, c, zl: (x, zh, y, c, (zl + 3) % 6))


def triple_shift(value, step):
    return permute(
        value, lambda x, zh, y, c, zl: (x, zh, y, c, zl // 3 * 3 + (zl + step) % 3)
    )


def x_swap(value, which):
    goal = {"even": (1, 0, 3, 2), "odd": (3, 2, 1, 0), "across": (2, 3, 0, 1)}[which]
    return permute(value, lambda x, zh, y, c, zl: (goal[x], zh, y, c, zl))


def gather(value, axes, count):
    copies = jnp.broadcast_to(value[None], (count,) + value.shape)
    return lax.all_to_all(copies, axes, 0, 0, tiled=True).reshape(-1, value.shape[1])


def after(value, *others):
    return lax.optimization_barrier((value,) + others)[0]


def neighbours_x(block):
    return [x_swap(block, which) for which in ("even", "odd", "across")]


def in_order_x(block, even, odd, across):
    x = lax.axis_index("x")
    whole = jnp.zeros((4,) + block.shape, block.dtype)
    for value, at in ((block, x), (even, x ^ 1), (odd, 3 - x), (across, (x + 2) % 4)):
        whole = lax.dynamic_update_slice_in_dim(whole, value[None], at, 0)
    return whole.reshape(-1, block.shape[1])


def attend_kernel(place_ref, length_ref, temp_ref, frames, own_w, other_w, *refs):
    tails, (out_ref, x_buf, w_buf, qkv, sems) = refs[:6], refs[6:]
    core, place = place_ref[0], place_ref[1]
    base, within = place // 3 * 3, lax.rem(place, 3)
    below, above = lax.rem(within + 2, 3), lax.rem(within + 1, 3)
    slots = (
        place,
        base + below,
        base + above,
        3 - base + within,
        3 - base + below,
        3 - base + above,
    )
    tail = tails[0].shape[0]
    head = frames.shape[0] // 6
    copies = []
    for number in range(4):
        rows = pl.ds(number * 384, 384)
        for source, half in ((own_w, core), (other_w, 1 - core)):
            columns = pl.ds(pl.multiple_of(half * 384, 128), 384)
            copies.append((source.at[rows], w_buf.at[rows, columns]))
    for number, slot in enumerate(slots):
        rows = pl.ds(number * (head + tail), head)
        copies.append((frames.at[pl.ds(number * head, head)], x_buf.at[rows]))
        rows = pl.ds(pl.multiple_of(slot * (head + tail) + head, tail), tail)
        copies.append((tails[number], x_buf.at[rows]))
    copies = [
        pltpu.make_async_copy(source, goal, sems.at[number])
        for number, (source, goal) in enumerate(copies)
    ]
    for copy in copies:
        copy.start()
    for copy in copies:
        copy.wait()
    qkv[...] = jnp.dot(
        x_buf[...], w_buf[...], preferred_element_type=jnp.float32
    ).astype(jnp.bfloat16)

    total = x_buf.shape[0]
    live = lax.broadcasted_iota(jnp.int32, (total, 1), 0) < length_ref[0]
    lane = lax.broadcasted_iota(jnp.int32, (total, 128), 1)
    place = lax.broadcasted_iota(jnp.int32, (1, 2 * total), 1)
    for two in range(2):
        query, key_part, value = (
            qkv[:, two * 384 + k * 128 : two * 384 + k * 128 + 128] for k in range(3)
        )
        none = jnp.zeros_like(query)
        query = jnp.concatenate(
            [jnp.where(lane < HD, query, none), jnp.where(lane < HD, none, query)]
        )
        scores = lax.dot_general(
            key_part, query, (((1,), (1,)), ((), ())), preferred_element_type=jnp.float32
        )
        scale = jnp.where(place < total, temp_ref[2 * two] / 8.0, temp_ref[2 * two + 1] / 8.0)
        scores = jnp.where(live, scores * scale, -1e30)
        scores = jnp.exp(scores - jnp.max(scores, axis=0, keepdims=True))
        mixed = lax.dot_general(
            value,
            scores.astype(jnp.bfloat16),
            (((0,), (0,)), ((), ())),
            preferred_element_type=jnp.float32,
        )
        mixed = mixed / jnp.sum(scores, axis=0, keepdims=True)
        mixed = jnp.concatenate([mixed[:HD, :total], mixed[HD:, total:]]).T
        out_ref[:, :, two * 128 : two * 128 + 128] = mixed.astype(jnp.bfloat16).reshape(
            out_ref.shape[0], out_ref.shape[1], 128
        )


SMEM = pl.BlockSpec(memory_space=pltpu.SMEM)
VMEM = pl.BlockSpec(memory_space=pltpu.VMEM)
ANYWHERE = pl.BlockSpec(memory_space=pl.ANY)


def attend(place, length, temp, frames, own_w, other_w, tails):
    rows, width = frames.shape
    rows += 6 * tails[0].shape[0]
    return pl.pallas_call(
        attend_kernel,
        out_shape=jax.ShapeDtypeStruct((6, rows // 6, 256), jnp.bfloat16),
        in_specs=[SMEM] * 3 + [ANYWHERE] * 9,
        out_specs=VMEM,
        scratch_shapes=[
            pltpu.VMEM((rows, width), jnp.bfloat16),
            pltpu.VMEM((width, 768), jnp.bfloat16),
            pltpu.VMEM((rows, 768), jnp.bfloat16),
            pltpu.SemaphoreType.DMA((20,)),
        ],
        compiler_params=pltpu.CompilerParams(vmem_limit_bytes=58 * 2**20),
        cost_estimate=pl.CostEstimate(
            flops=3 * 10**9, bytes_accessed=5 * 10**6, transcendentals=2 * 10**6
        ),
    )(place, length, temp, frames, own_w, other_w, *tails)


def turned_half(heads_ref, which):
    first = jnp.concatenate([heads_ref[at, :, :128] for at in range(6)], axis=1)
    second = jnp.concatenate([heads_ref[at, :, 128:] for at in range(6)], axis=1)
    return jnp.where(which == 0, first, second).T


def project_half_kernel(place_ref, heads_ref, own_any, out_ref, own_ref, sems):
    parts = [pl.ds(number * 384, 384) for number in range(4)]
    copies = [
        pltpu.make_async_copy(own_any.at[rows], own_ref.at[rows], sems.at[number])
        for number, rows in enumerate(parts)
    ]
    for copy in copies:
        copy.start()
    mine = turned_half(heads_ref, place_ref[0])
    for copy, rows in zip(copies, parts):
        copy.wait()
        out_ref[rows] = jnp.dot(own_ref[rows], mine, preferred_element_type=jnp.float32)


def project_kernel(place_ref, heads_ref, *refs):
    others, (sums_ref, out_ref, total) = refs[:4], refs[4:]
    given = turned_half(heads_ref, 1 - place_ref[0])
    for number, other in enumerate(others):
        rows = pl.ds(number * 384, 384)
        total[rows] = sums_ref[rows] + jnp.dot(
            other[...], given, preferred_element_type=jnp.float32
        )
    for x in range(4):
        pieces = []
        for zh in range(2):
            for y in range(8):
                at = ((y * 4 + x) * 2 + zh) * 24
                pieces.append(total[at : at + 24, :])
        block = jnp.concatenate(pieces).T
        out_ref[:, x * 384 : x * 384 + 384] = block.astype(jnp.bfloat16)


def project_half(place, heads, own):
    return pl.pallas_call(
        project_half_kernel,
        out_shape=jax.ShapeDtypeStruct((own.shape[0], heads.shape[1]), jnp.float32),
        in_specs=[SMEM, VMEM, ANYWHERE],
        out_specs=VMEM,
        scratch_shapes=[pltpu.VMEM(own.shape, jnp.bfloat16), pltpu.SemaphoreType.DMA((4,))],
        compiler_params=pltpu.CompilerParams(vmem_limit_bytes=16 * 2**20),
        cost_estimate=pl.CostEstimate(
            flops=3 * 10**8, bytes_accessed=3 * 10**6, transcendentals=0
        ),
    )(place, heads, own)


def project(place, heads, others, sums):
    return pl.pallas_call(
        project_kernel,
        out_shape=jax.ShapeDtypeStruct((heads.shape[1], 1536), jnp.bfloat16),
        in_specs=[SMEM] + [VMEM] * 6,
        out_specs=VMEM,
        scratch_shapes=[pltpu.VMEM(sums.shape, jnp.float32)],
        compiler_params=pltpu.CompilerParams(vmem_limit_bytes=16 * 2**20),
        cost_estimate=pl.CostEstimate(
            flops=3 * 10**8, bytes_accessed=4 * 10**6, transcendentals=0
        ),
    )(place, heads, *others, sums)


def on_device(latents, norm_gain, w_qkv, w_out, head_temp, lengths):
    frames = latents[0]
    values = frames.astype(jnp.float32)
    rms = jnp.sqrt(jnp.mean(values * values, axis=-1, keepdims=True) + 1e-06)
    normed = (values / rms * norm_gain).astype(jnp.bfloat16)
    head = 3 * normed.shape[0] // 4
    whole = lax.all_gather(normed[:head], "zl", axis=0, tiled=True)
    tail = normed[head:]
    far = other_triple(tail)
    near = [triple_shift(tail, 1), triple_shift(tail, 2)]

    rows = w_qkv.reshape(3, 12, 2, 128).transpose(2, 1, 0, 3).reshape(2, 12, 384)
    columns = w_out.T.reshape(12, 2, 128).transpose(1, 0, 2)
    both = jnp.concatenate([rows, columns], axis=2).reshape(1, 2, 48, 128)
    both = jnp.broadcast_to(both, (12, 2, 48, 128)).reshape(24, 48, 128)
    both = lax.all_to_all(both, ("zh", "zl", "c"), 0, 0, tiled=True)
    both, far, near = lax.optimization_barrier((both, far, near))
    both = both.reshape(2, 6, 2, 12, 512)
    rows = lax.dynamic_index_in_dim(both[..., :384], lax.axis_index("zl"), 1, keepdims=False)
    rows = rows.reshape(48, 384)
    by_y = gather(rows, "y", 8)
    columns = both[..., 384:].transpose(0, 2, 3, 1, 4).reshape(48, 768)
    by_y, others = lax.optimization_barrier((by_y, neighbours_x(columns)))
    by_y = by_y.reshape(8, 2, 24, 384).transpose(1, 0, 2, 3).reshape(384, 384)
    out_by_x = in_order_x(columns, *others)
    own_w = gather(by_y, "x", 4)
    beyond = [triple_shift(far, 1), triple_shift(far, 2)]
    own_w, beyond = lax.optimization_barrier((own_w, beyond))
    other_w = other_core(own_w)
    out_own = lax.all_gather(out_by_x, "y", axis=0, tiled=True)

    place = jnp.stack([lax.axis_index("c"), lax.axis_index("zl")]).astype(jnp.int32)
    tails = [tail] + near + [far] + beyond
    blocks = attend(place, lengths, head_temp, whole, own_w, other_w, tails)
    own = lax.all_to_all(blocks, "zl", 0, 0, tiled=True)
    out_own, one_head = lax.optimization_barrier((out_own, blocks[0, :1, 0].astype(jnp.float32)))
    place += (one_head * 0.0).astype(jnp.int32)
    out_others = [other_core(out_own[at : at + 384]) for at in range(0, 1536, 384)]
    sums = project_half(place, own, out_own)
    return project(place, own, out_others, sums)[None]


def solution(mesh):
    split = Mesh(mesh.devices.reshape(SIZES), AXES)
    clip = ("x", "zh", "y", "c")
    in_specs = (
        P(clip, "zl", None),
        P(),
        P(None, clip, "zl"),
        P("zl", clip),
        P("zl"),
        P(clip),
    )
    out_specs = P(clip, "zl", None)
    return jax.shard_map(
        on_device, mesh=split, in_specs=in_specs, out_specs=out_specs, check_vma=False
    )
```

```python
import functools

import jax
import jax.numpy as jnp
import numpy as np
from jax import lax
from jax.experimental import pallas as pl
from jax.experimental.pallas import tpu as pltpu
from jax.sharding import Mesh, PartitionSpec as P

HD = 64
AXES = ("x", "zh", "y", "c", "zl")
SIZES = (4, 2, 8, 2, 6)


def permute(value, move):
    pairs = []
    for place in np.ndindex(*SIZES):
        goal = move(*place)
        if goal is not None:
            pairs.append(
                (int(np.ravel_multi_index(place, SIZES)), int(np.ravel_multi_index(goal, SIZES)))
            )
    return lax.ppermute(value, AXES, pairs)


def other_core(value):
    return permute(value, lambda x, zh, y, c, zl: (x, zh, y, 1 - c, zl))


def x_swap(value, which):
    goal = {"even": (1, 0, 3, 2), "odd": (3, 2, 1, 0), "across": (2, 3, 0, 1)}[which]
    return permute(value, lambda x, zh, y, c, zl: (goal[x], zh, y, c, zl))


def gather(value, axes, count):
    copies = jnp.broadcast_to(value[None], (count,) + value.shape)
    return lax.all_to_all(copies, axes, 0, 0, tiled=True).reshape(-1, value.shape[1])


def after(value, *others):
    return lax.optimization_barrier((value,) + others)[0]


def gather_x(block):
    x = lax.axis_index("x")
    whole = jnp.zeros((4,) + block.shape, block.dtype)
    for value, at in (
        (block, x),
        (x_swap(block, "even"), x ^ 1),
        (x_swap(block, "odd"), 3 - x),
        (x_swap(block, "across"), (x + 2) % 4),
    ):
        whole = lax.dynamic_update_slice_in_dim(whole, value[None], at, 0)
    return whole.reshape(-1, block.shape[1])


def attend_kernel(core_ref, length_ref, temp_ref, frames, own_w, other_w, *refs):
    out_ref, x_buf, w_buf, qkv, sems = refs
    core = core_ref[0]
    copies = []
    for number in range(4):
        rows = pl.ds(number * 384, 384)
        for source, half in ((own_w, core), (other_w, 1 - core)):
            columns = pl.ds(pl.multiple_of(half * 384, 128), 384)
            copies.append((source.at[rows], w_buf.at[rows, columns]))
    for number in range(6):
        rows = pl.ds(number * 128, 128)
        copies.append((frames.at[rows], x_buf.at[rows]))
    copies = [
        pltpu.make_async_copy(source, goal, sems.at[number])
        for number, (source, goal) in enumerate(copies)
    ]
    for copy in copies:
        copy.start()
    for copy in copies:
        copy.wait()
    qkv[...] = jnp.dot(
        x_buf[...], w_buf[...], preferred_element_type=jnp.float32
    ).astype(jnp.bfloat16)

    total = x_buf.shape[0]
    live = lax.broadcasted_iota(jnp.int32, (total, 1), 0) < length_ref[0]
    lane = lax.broadcasted_iota(jnp.int32, (total, 128), 1)
    place = lax.broadcasted_iota(jnp.int32, (1, 2 * total), 1)
    for two in range(2):
        query, key_part, value = (
            qkv[:, two * 384 + k * 128 : two * 384 + k * 128 + 128] for k in range(3)
        )
        none = jnp.zeros_like(query)
        query = jnp.concatenate(
            [jnp.where(lane < HD, query, none), jnp.where(lane < HD, none, query)]
        )
        scores = lax.dot_general(
            key_part, query, (((1,), (1,)), ((), ())), preferred_element_type=jnp.float32
        )
        scale = jnp.where(place < total, temp_ref[2 * two] / 8.0, temp_ref[2 * two + 1] / 8.0)
        scores = jnp.where(live, scores * scale, -1e30)
        scores = jnp.exp(scores - jnp.max(scores, axis=0, keepdims=True))
        mixed = lax.dot_general(
            value,
            scores.astype(jnp.bfloat16),
            (((0,), (0,)), ((), ())),
            preferred_element_type=jnp.float32,
        )
        mixed = mixed / jnp.sum(scores, axis=0, keepdims=True)
        mixed = jnp.concatenate([mixed[:HD, :total], mixed[HD:, total:]]).T
        out_ref[:, :, two * 128 : two * 128 + 128] = mixed.astype(jnp.bfloat16).reshape(
            out_ref.shape[0], out_ref.shape[1], 128
        )


SMEM = pl.BlockSpec(memory_space=pltpu.SMEM)
VMEM = pl.BlockSpec(memory_space=pltpu.VMEM)
ANYWHERE = pl.BlockSpec(memory_space=pl.ANY)


def attend(core, length, temp, frames, own_w, other_w):
    rows, width = frames.shape
    return pl.pallas_call(
        attend_kernel,
        out_shape=jax.ShapeDtypeStruct((6, rows // 6, 256), jnp.bfloat16),
        in_specs=[SMEM] * 3 + [ANYWHERE] * 3,
        out_specs=VMEM,
        scratch_shapes=[
            pltpu.VMEM((rows, width), jnp.bfloat16),
            pltpu.VMEM((width, 768), jnp.bfloat16),
            pltpu.VMEM((rows, 768), jnp.bfloat16),
            pltpu.SemaphoreType.DMA((14,)),
        ],
        compiler_params=pltpu.CompilerParams(vmem_limit_bytes=50 * 2**20),
        cost_estimate=pl.CostEstimate(
            flops=3 * 10**9, bytes_accessed=5 * 10**6, transcendentals=2 * 10**6
        ),
    )(core, length, temp, frames, own_w, other_w)


def turned_half(heads_ref, which):
    first = jnp.concatenate([heads_ref[at, :, :128] for at in range(6)], axis=1)
    second = jnp.concatenate([heads_ref[at, :, 128:] for at in range(6)], axis=1)
    return jnp.where(which == 0, first, second).T


def project_half_kernel(place_ref, heads_ref, own_any, out_ref, own_ref, sems):
    parts = [pl.ds(number * 384, 384) for number in range(4)]
    copies = [
        pltpu.make_async_copy(own_any.at[rows], own_ref.at[rows], sems.at[number])
        for number, rows in enumerate(parts)
    ]
    for copy in copies:
        copy.start()
    mine = turned_half(heads_ref, place_ref[0])
    for copy, rows in zip(copies, parts):
        copy.wait()
        out_ref[rows] = jnp.dot(own_ref[rows], mine, preferred_element_type=jnp.float32)


def project_kernel(place_ref, heads_ref, other_ref, sums_ref, out_ref, total):
    given = turned_half(heads_ref, 1 - place_ref[0])
    total[...] = sums_ref[...] + jnp.dot(
        other_ref[...], given, preferred_element_type=jnp.float32
    )
    for x in range(4):
        pieces = []
        for zh in range(2):
            for y in range(8):
                at = ((y * 4 + x) * 2 + zh) * 24
                pieces.append(total[at : at + 24, :])
        block = jnp.concatenate(pieces).T
        out_ref[:, x * 384 : x * 384 + 384] = block.astype(jnp.bfloat16)


def project_half(place, heads, own):
    return pl.pallas_call(
        project_half_kernel,
        out_shape=jax.ShapeDtypeStruct((own.shape[0], heads.shape[1]), jnp.float32),
        in_specs=[SMEM, VMEM, ANYWHERE],
        out_specs=VMEM,
        scratch_shapes=[pltpu.VMEM(own.shape, jnp.bfloat16), pltpu.SemaphoreType.DMA((4,))],
        compiler_params=pltpu.CompilerParams(vmem_limit_bytes=16 * 2**20),
        cost_estimate=pl.CostEstimate(
            flops=3 * 10**8, bytes_accessed=3 * 10**6, transcendentals=0
        ),
    )(place, heads, own)


def project(place, heads, other, sums):
    return pl.pallas_call(
        project_kernel,
        out_shape=jax.ShapeDtypeStruct((heads.shape[1], 1536), jnp.bfloat16),
        in_specs=[SMEM] + [VMEM] * 3,
        out_specs=VMEM,
        scratch_shapes=[pltpu.VMEM(sums.shape, jnp.float32)],
        compiler_params=pltpu.CompilerParams(vmem_limit_bytes=16 * 2**20),
        cost_estimate=pl.CostEstimate(
            flops=3 * 10**8, bytes_accessed=4 * 10**6, transcendentals=0
        ),
    )(place, heads, other, sums)


def on_device(latents, norm_gain, w_qkv, w_out, head_temp, lengths):
    frames = latents[0]
    values = frames.astype(jnp.float32)
    rms = jnp.sqrt(jnp.mean(values * values, axis=-1, keepdims=True) + 1e-06)
    normed = (values / rms * norm_gain).astype(jnp.bfloat16)
    whole = lax.all_gather(normed, "zl", axis=0, tiled=True)

    rows = w_qkv.reshape(3, 12, 2, 128).transpose(2, 1, 0, 3).reshape(2, 12, 384)
    columns = w_out.T.reshape(12, 2, 128).transpose(1, 0, 2)
    both = jnp.concatenate([rows, columns], axis=2).reshape(1, 2, 48, 128)
    both = jnp.broadcast_to(both, (12, 2, 48, 128)).reshape(24, 48, 128)
    both = lax.all_to_all(after(both, normed), ("zh", "zl", "c"), 0, 0, tiled=True)
    both = both.reshape(2, 6, 2, 12, 512)
    rows = lax.dynamic_index_in_dim(both[..., :384], lax.axis_index("zl"), 1, keepdims=False)
    rows = rows.reshape(48, 384)
    by_y = gather(rows, "y", 8).reshape(8, 2, 24, 384).transpose(1, 0, 2, 3).reshape(384, 384)
    columns = both[..., 384:].transpose(0, 2, 3, 1, 4).reshape(48, 768)
    own_w = gather(by_y, "x", 4)
    out_by_x, own_w = lax.optimization_barrier((gather_x(columns), own_w))
    other_w = other_core(own_w)
    out_own = lax.all_gather(out_by_x, "y", axis=0, tiled=True)

    core = lax.axis_index("c").reshape(1).astype(jnp.int32)
    blocks = attend(core, lengths, head_temp, whole, own_w, other_w)
    own = lax.all_to_all(blocks, "zl", 0, 0, tiled=True)
    own, out_own = lax.optimization_barrier((own, out_own))
    out_other = other_core(out_own)
    sums = project_half(core, own, out_own)
    return project(core, own, out_other, sums)[None]


def solution(mesh):
    split = Mesh(mesh.devices.reshape(SIZES), AXES)
    clip = ("x", "zh", "y", "c")
    in_specs = (
        P(clip, "zl", None),
        P(),
        P(None, clip, "zl"),
        P("zl", clip),
        P("zl"),
        P(clip),
    )
    out_specs = P(clip, "zl", None)
    return jax.shard_map(
        on_device, mesh=split, in_specs=in_specs, out_specs=out_specs, check_vma=False
    )
```

```python
import functools

import jax
import jax.numpy as jnp
import numpy as np
from jax import lax
from jax.experimental import pallas as pl
from jax.experimental.pallas import tpu as pltpu
from jax.sharding import Mesh, PartitionSpec as P

HD = 64
AXES = ("x", "zh", "y", "c", "zl")
SIZES = (4, 2, 8, 2, 6)


def permute(value, move):
    pairs = []
    for place in np.ndindex(*SIZES):
        goal = move(*place)
        if goal is not None:
            pairs.append(
                (int(np.ravel_multi_index(place, SIZES)), int(np.ravel_multi_index(goal, SIZES)))
            )
    return lax.ppermute(value, AXES, pairs)


def other_core(value):
    return permute(value, lambda x, zh, y, c, zl: (x, zh, y, 1 - c, zl))


def x_swap(value, which):
    goal = {"even": (1, 0, 3, 2), "odd": (3, 2, 1, 0), "across": (2, 3, 0, 1)}[which]
    return permute(value, lambda x, zh, y, c, zl: (goal[x], zh, y, c, zl))


def gather(value, axes, count):
    copies = jnp.broadcast_to(value[None], (count,) + value.shape)
    return lax.all_to_all(copies, axes, 0, 0, tiled=True).reshape(-1, value.shape[1])


def after(value, *others):
    return lax.optimization_barrier((value,) + others)[0]


def gather_x(block):
    x = lax.axis_index("x")
    whole = jnp.zeros((4,) + block.shape, block.dtype)
    for value, at in (
        (block, x),
        (x_swap(block, "even"), x ^ 1),
        (x_swap(block, "odd"), 3 - x),
        (x_swap(block, "across"), (x + 2) % 4),
    ):
        whole = lax.dynamic_update_slice_in_dim(whole, value[None], at, 0)
    return whole.reshape(-1, block.shape[1])


def attend_kernel(core_ref, length_ref, temp_ref, frames, own_w, other_w, *refs):
    out_ref, x_buf, w_buf, qkv, sems = refs
    core = core_ref[0]
    copies = []
    for number in range(4):
        rows = pl.ds(number * 384, 384)
        for source, half in ((own_w, core), (other_w, 1 - core)):
            columns = pl.ds(pl.multiple_of(half * 384, 128), 384)
            copies.append((source.at[rows], w_buf.at[rows, columns]))
    for number in range(6):
        rows = pl.ds(number * 128, 128)
        copies.append((frames.at[rows], x_buf.at[rows]))
    copies = [
        pltpu.make_async_copy(source, goal, sems.at[number])
        for number, (source, goal) in enumerate(copies)
    ]
    for copy in copies:
        copy.start()
    for copy in copies:
        copy.wait()
    qkv[...] = jnp.dot(
        x_buf[...], w_buf[...], preferred_element_type=jnp.float32
    ).astype(jnp.bfloat16)

    total = x_buf.shape[0]
    live = lax.broadcasted_iota(jnp.int32, (total, 1), 0) < length_ref[0]
    lane = lax.broadcasted_iota(jnp.int32, (total, 128), 1)
    place = lax.broadcasted_iota(jnp.int32, (1, 2 * total), 1)
    for two in range(2):
        query, key_part, value = (
            qkv[:, two * 384 + k * 128 : two * 384 + k * 128 + 128] for k in range(3)
        )
        none = jnp.zeros_like(query)
        query = jnp.concatenate(
            [jnp.where(lane < HD, query, none), jnp.where(lane < HD, none, query)]
        )
        scores = lax.dot_general(
            key_part, query, (((1,), (1,)), ((), ())), preferred_element_type=jnp.float32
        )
        scale = jnp.where(place < total, temp_ref[2 * two] / 8.0, temp_ref[2 * two + 1] / 8.0)
        scores = jnp.where(live, scores * scale, -1e30)
        scores = jnp.exp(scores - jnp.max(scores, axis=0, keepdims=True))
        mixed = lax.dot_general(
            value,
            scores.astype(jnp.bfloat16),
            (((0,), (0,)), ((), ())),
            preferred_element_type=jnp.float32,
        )
        mixed = mixed / jnp.sum(scores, axis=0, keepdims=True)
        mixed = jnp.concatenate([mixed[:HD, :total], mixed[HD:, total:]]).T
        out_ref[:, :, two * 128 : two * 128 + 128] = mixed.astype(jnp.bfloat16).reshape(
            out_ref.shape[0], out_ref.shape[1], 128
        )


SMEM = pl.BlockSpec(memory_space=pltpu.SMEM)
VMEM = pl.BlockSpec(memory_space=pltpu.VMEM)
ANYWHERE = pl.BlockSpec(memory_space=pl.ANY)


def attend(core, length, temp, frames, own_w, other_w):
    rows, width = frames.shape
    return pl.pallas_call(
        attend_kernel,
        out_shape=jax.ShapeDtypeStruct((6, rows // 6, 256), jnp.bfloat16),
        in_specs=[SMEM] * 3 + [ANYWHERE] * 3,
        out_specs=VMEM,
        scratch_shapes=[
            pltpu.VMEM((rows, width), jnp.bfloat16),
            pltpu.VMEM((width, 768), jnp.bfloat16),
            pltpu.VMEM((rows, 768), jnp.bfloat16),
            pltpu.SemaphoreType.DMA((14,)),
        ],
        compiler_params=pltpu.CompilerParams(vmem_limit_bytes=50 * 2**20),
        cost_estimate=pl.CostEstimate(
            flops=3 * 10**9, bytes_accessed=5 * 10**6, transcendentals=2 * 10**6
        ),
    )(core, length, temp, frames, own_w, other_w)


def turned_half(heads_ref, which):
    first = jnp.concatenate([heads_ref[at, :, :128] for at in range(6)], axis=1)
    second = jnp.concatenate([heads_ref[at, :, 128:] for at in range(6)], axis=1)
    return jnp.where(which == 0, first, second).T


def project_half_kernel(place_ref, heads_ref, own_any, out_ref, own_ref, sems):
    parts = [pl.ds(number * 384, 384) for number in range(4)]
    copies = [
        pltpu.make_async_copy(own_any.at[rows], own_ref.at[rows], sems.at[number])
        for number, rows in enumerate(parts)
    ]
    for copy in copies:
        copy.start()
    mine = turned_half(heads_ref, place_ref[0])
    for copy, rows in zip(copies, parts):
        copy.wait()
        out_ref[rows] = jnp.dot(own_ref[rows], mine, preferred_element_type=jnp.float32)


def project_kernel(place_ref, heads_ref, other_ref, sums_ref, out_ref, total):
    core = place_ref[0]
    given = turned_half(heads_ref, 1 - core)
    total[...] = jnp.dot(other_ref[...], given, preferred_element_type=jnp.float32)
    for x in range(4):
        pieces = []
        for zh in range(2):
            for y in range(8):
                own_y = jnp.where(core == 0, y, 7 - y)
                own_at = pl.multiple_of(((own_y * 4 + x) * 2 + zh) * 24, 8)
                other_at = pl.multiple_of((((7 - own_y) * 4 + x) * 2 + zh) * 24, 8)
                pieces.append(sums_ref[pl.ds(own_at, 24), :] + total[pl.ds(other_at, 24), :])
        block = jnp.concatenate(pieces).T
        out_ref[:, x * 384 : x * 384 + 384] = block.astype(jnp.bfloat16)


def project_half(place, heads, own):
    return pl.pallas_call(
        project_half_kernel,
        out_shape=jax.ShapeDtypeStruct((own.shape[0], heads.shape[1]), jnp.float32),
        in_specs=[SMEM, VMEM, ANYWHERE],
        out_specs=VMEM,
        scratch_shapes=[pltpu.VMEM(own.shape, jnp.bfloat16), pltpu.SemaphoreType.DMA((4,))],
        compiler_params=pltpu.CompilerParams(vmem_limit_bytes=16 * 2**20),
        cost_estimate=pl.CostEstimate(
            flops=3 * 10**8, bytes_accessed=3 * 10**6, transcendentals=0
        ),
    )(place, heads, own)


def project(place, heads, other, sums):
    return pl.pallas_call(
        project_kernel,
        out_shape=jax.ShapeDtypeStruct((heads.shape[1], 1536), jnp.bfloat16),
        in_specs=[SMEM] + [VMEM] * 3,
        out_specs=VMEM,
        scratch_shapes=[pltpu.VMEM(sums.shape, jnp.float32)],
        compiler_params=pltpu.CompilerParams(vmem_limit_bytes=16 * 2**20),
        cost_estimate=pl.CostEstimate(
            flops=3 * 10**8, bytes_accessed=4 * 10**6, transcendentals=0
        ),
    )(place, heads, other, sums)


def on_device(latents, norm_gain, w_qkv, w_out, head_temp, lengths):
    frames = latents[0]
    values = frames.astype(jnp.float32)
    rms = jnp.sqrt(jnp.mean(values * values, axis=-1, keepdims=True) + 1e-06)
    normed = (values / rms * norm_gain).astype(jnp.bfloat16)
    whole = lax.all_gather(normed, "zl", axis=0, tiled=True)

    rows = w_qkv.reshape(3, 12, 2, 128).transpose(2, 1, 0, 3).reshape(2, 12, 384)
    columns = w_out.T.reshape(12, 2, 128).transpose(1, 0, 2)
    both = jnp.concatenate([rows, columns], axis=2).reshape(1, 2, 48, 128)
    both = jnp.broadcast_to(both, (12, 2, 48, 128)).reshape(24, 48, 128)
    both = lax.all_to_all(after(both, normed), ("zh", "zl", "c"), 0, 0, tiled=True)
    both = both.reshape(2, 6, 2, 12, 512)
    rows = lax.dynamic_index_in_dim(both[..., :384], lax.axis_index("zl"), 1, keepdims=False)
    rows = rows.reshape(48, 384)
    by_y = gather(rows, "y", 8).reshape(8, 2, 24, 384).transpose(1, 0, 2, 3).reshape(384, 384)
    columns = both[..., 384:].transpose(0, 2, 3, 1, 4).reshape(48, 768)
    own_w = gather(by_y, "x", 4)
    out_by_x, own_w = lax.optimization_barrier((gather_x(columns), own_w))
    other_w = other_core(own_w)
    out_own = lax.all_gather(
        out_by_x,
        ("y", "c"),
        axis=0,
        tiled=True,
        axis_index_groups=[list(range(0, 16, 2)), list(range(15, 0, -2))],
    )

    core = lax.axis_index("c").reshape(1).astype(jnp.int32)
    blocks = attend(core, lengths, head_temp, whole, own_w, other_w)
    own = lax.all_to_all(blocks, "zl", 0, 0, tiled=True)
    own, out_own = lax.optimization_barrier((own, out_own))
    out_other = other_core(out_own)
    sums = project_half(core, own, out_own)
    return project(core, own, out_other, sums)[None]


def solution(mesh):
    split = Mesh(mesh.devices.reshape(SIZES), AXES)
    clip = ("x", "zh", "y", "c")
    in_specs = (
        P(clip, "zl", None),
        P(),
        P(None, clip, "zl"),
        P("zl", clip),
        P("zl"),
        P(clip),
    )
    out_specs = P(clip, "zl", None)
    return jax.shard_map(
        on_device, mesh=split, in_specs=in_specs, out_specs=out_specs, check_vma=False
    )
```

```python
import functools

import jax
import jax.numpy as jnp
import numpy as np
from jax import lax
from jax.experimental import pallas as pl
from jax.experimental.pallas import tpu as pltpu
from jax.sharding import Mesh, PartitionSpec as P

HD = 64
AXES = ("x", "zh", "y", "c", "zl")
SIZES = (4, 2, 8, 2, 6)


def permute(value, move):
    pairs = []
    for place in np.ndindex(*SIZES):
        goal = move(*place)
        if goal is not None:
            pairs.append(
                (int(np.ravel_multi_index(place, SIZES)), int(np.ravel_multi_index(goal, SIZES)))
            )
    return lax.ppermute(value, AXES, pairs)


def other_core(value):
    return permute(value, lambda x, zh, y, c, zl: (x, zh, y, 1 - c, zl))


def x_swap(value, which):
    goal = {"even": (1, 0, 3, 2), "odd": (3, 2, 1, 0), "across": (2, 3, 0, 1)}[which]
    return permute(value, lambda x, zh, y, c, zl: (goal[x], zh, y, c, zl))


def gather(value, axes, count):
    copies = jnp.broadcast_to(value[None], (count,) + value.shape)
    return lax.all_to_all(copies, axes, 0, 0, tiled=True).reshape(-1, value.shape[1])


def after(value, *others):
    return lax.optimization_barrier((value,) + others)[0]


def gather_x(block):
    x = lax.axis_index("x")
    whole = jnp.zeros((4,) + block.shape, block.dtype)
    for value, at in (
        (block, x),
        (x_swap(block, "even"), x ^ 1),
        (x_swap(block, "odd"), 3 - x),
        (x_swap(block, "across"), (x + 2) % 4),
    ):
        whole = lax.dynamic_update_slice_in_dim(whole, value[None], at, 0)
    return whole.reshape(-1, block.shape[1])


def attend_kernel(core_ref, length_ref, temp_ref, frames, own_w, other_w, *refs):
    out_ref, x_buf, w_buf, qkv, sems = refs
    core = core_ref[0]
    copies = []
    for number in range(4):
        rows = pl.ds(number * 384, 384)
        for source, half in ((own_w, core), (other_w, 1 - core)):
            columns = pl.ds(pl.multiple_of(half * 384, 128), 384)
            copies.append((source.at[rows], w_buf.at[rows, columns]))
    for number in range(6):
        rows = pl.ds(number * 128, 128)
        copies.append((frames.at[rows], x_buf.at[rows]))
    copies = [
        pltpu.make_async_copy(source, goal, sems.at[number])
        for number, (source, goal) in enumerate(copies)
    ]
    for copy in copies:
        copy.start()
    for copy in copies:
        copy.wait()
    qkv[...] = jnp.dot(
        x_buf[...], w_buf[...], preferred_element_type=jnp.float32
    ).astype(jnp.bfloat16)

    total = x_buf.shape[0]
    live = lax.broadcasted_iota(jnp.int32, (total, 1), 0) < length_ref[0]
    lane = lax.broadcasted_iota(jnp.int32, (total, 128), 1)
    place = lax.broadcasted_iota(jnp.int32, (1, 2 * total), 1)
    for two in range(2):
        query, key_part, value = (
            qkv[:, two * 384 + k * 128 : two * 384 + k * 128 + 128] for k in range(3)
        )
        none = jnp.zeros_like(query)
        query = jnp.concatenate(
            [jnp.where(lane < HD, query, none), jnp.where(lane < HD, none, query)]
        )
        scores = lax.dot_general(
            key_part, query, (((1,), (1,)), ((), ())), preferred_element_type=jnp.float32
        )
        scale = jnp.where(place < total, temp_ref[2 * two] / 8.0, temp_ref[2 * two + 1] / 8.0)
        scores = jnp.where(live, scores * scale, -1e30)
        scores = jnp.exp(scores - jnp.max(scores, axis=0, keepdims=True))
        mixed = lax.dot_general(
            value,
            scores.astype(jnp.bfloat16),
            (((0,), (0,)), ((), ())),
            preferred_element_type=jnp.float32,
        )
        mixed = mixed / jnp.sum(scores, axis=0, keepdims=True)
        mixed = jnp.concatenate([mixed[:HD, :total], mixed[HD:, total:]]).T
        out_ref[:, :, two * 128 : two * 128 + 128] = mixed.astype(jnp.bfloat16).reshape(
            out_ref.shape[0], out_ref.shape[1], 128
        )


SMEM = pl.BlockSpec(memory_space=pltpu.SMEM)
VMEM = pl.BlockSpec(memory_space=pltpu.VMEM)
ANYWHERE = pl.BlockSpec(memory_space=pl.ANY)


def attend(core, length, temp, frames, own_w, other_w):
    rows, width = frames.shape
    return pl.pallas_call(
        attend_kernel,
        out_shape=jax.ShapeDtypeStruct((6, rows // 6, 256), jnp.bfloat16),
        in_specs=[SMEM] * 3 + [ANYWHERE] * 3,
        out_specs=VMEM,
        scratch_shapes=[
            pltpu.VMEM((rows, width), jnp.bfloat16),
            pltpu.VMEM((width, 768), jnp.bfloat16),
            pltpu.VMEM((rows, 768), jnp.bfloat16),
            pltpu.SemaphoreType.DMA((14,)),
        ],
        compiler_params=pltpu.CompilerParams(vmem_limit_bytes=50 * 2**20),
        cost_estimate=pl.CostEstimate(
            flops=3 * 10**9, bytes_accessed=5 * 10**6, transcendentals=2 * 10**6
        ),
    )(core, length, temp, frames, own_w, other_w)


def turned_half(heads_ref, which):
    first = jnp.concatenate([heads_ref[at, :, :128] for at in range(6)], axis=1)
    second = jnp.concatenate([heads_ref[at, :, 128:] for at in range(6)], axis=1)
    return jnp.where(which == 0, first, second).T


def project_half_kernel(place_ref, heads_ref, own_any, out_ref, own_ref, sems):
    parts = [pl.ds(number * 384, 384) for number in range(4)]
    copies = [
        pltpu.make_async_copy(own_any.at[rows], own_ref.at[rows], sems.at[number])
        for number, rows in enumerate(parts)
    ]
    for copy in copies:
        copy.start()
    mine = turned_half(heads_ref, place_ref[0])
    for copy, rows in zip(copies, parts):
        copy.wait()
        out_ref[rows] = jnp.dot(own_ref[rows], mine, preferred_element_type=jnp.float32)


def project_kernel(place_ref, heads_ref, other_ref, sums_ref, out_ref, total):
    given = turned_half(heads_ref, 1 - place_ref[0])
    total[...] = sums_ref[...] + jnp.dot(
        other_ref[...], given, preferred_element_type=jnp.float32
    )
    for x in range(4):
        pieces = []
        for zh in range(2):
            for y in range(8):
                at = ((y * 4 + x) * 2 + zh) * 24
                pieces.append(total[at : at + 24, :])
        block = jnp.concatenate(pieces).T
        out_ref[:, x * 384 : x * 384 + 384] = block.astype(jnp.bfloat16)


def project_half(place, heads, own):
    return pl.pallas_call(
        project_half_kernel,
        out_shape=jax.ShapeDtypeStruct((own.shape[0], heads.shape[1]), jnp.float32),
        in_specs=[SMEM, VMEM, ANYWHERE],
        out_specs=VMEM,
        scratch_shapes=[pltpu.VMEM(own.shape, jnp.bfloat16), pltpu.SemaphoreType.DMA((4,))],
        compiler_params=pltpu.CompilerParams(vmem_limit_bytes=16 * 2**20),
        cost_estimate=pl.CostEstimate(
            flops=3 * 10**8, bytes_accessed=3 * 10**6, transcendentals=0
        ),
    )(place, heads, own)


def project(place, heads, other, sums):
    return pl.pallas_call(
        project_kernel,
        out_shape=jax.ShapeDtypeStruct((heads.shape[1], 1536), jnp.bfloat16),
        in_specs=[SMEM] + [VMEM] * 3,
        out_specs=VMEM,
        scratch_shapes=[pltpu.VMEM(sums.shape, jnp.float32)],
        compiler_params=pltpu.CompilerParams(vmem_limit_bytes=16 * 2**20),
        cost_estimate=pl.CostEstimate(
            flops=3 * 10**8, bytes_accessed=4 * 10**6, transcendentals=0
        ),
    )(place, heads, other, sums)


def normalise_kernel(frames_ref, gain_ref, out_ref):
    values = frames_ref[...].astype(jnp.float32)
    rms = jnp.sqrt(jnp.mean(values * values, axis=-1, keepdims=True) + 1e-06)
    out_ref[...] = (values / rms * gain_ref[...]).astype(jnp.bfloat16)


def normalise(frames, gain):
    return pl.pallas_call(
        normalise_kernel,
        out_shape=jax.ShapeDtypeStruct(frames.shape, jnp.bfloat16),
        in_specs=[VMEM] * 2,
        out_specs=VMEM,
        compiler_params=pltpu.CompilerParams(vmem_limit_bytes=8 * 2**20),
        cost_estimate=pl.CostEstimate(
            flops=10**6, bytes_accessed=8 * 10**5, transcendentals=0
        ),
    )(frames, gain[None])


def on_device(latents, norm_gain, w_qkv, w_out, head_temp, lengths):
    normed = normalise(latents[0], norm_gain)
    whole = lax.all_gather(normed, "zl", axis=0, tiled=True)

    rows = w_qkv.reshape(3, 12, 2, 128).transpose(2, 1, 0, 3).reshape(2, 12, 384)
    columns = w_out.T.reshape(12, 2, 128).transpose(1, 0, 2)
    both = jnp.concatenate([rows, columns], axis=2).reshape(1, 2, 48, 128)
    both = jnp.broadcast_to(both, (12, 2, 48, 128)).reshape(24, 48, 128)
    both = lax.all_to_all(after(both, normed), ("zh", "zl", "c"), 0, 0, tiled=True)
    both = both.reshape(2, 6, 2, 12, 512)
    rows = lax.dynamic_index_in_dim(both[..., :384], lax.axis_index("zl"), 1, keepdims=False)
    rows = rows.reshape(48, 384)
    by_y = gather(rows, "y", 8).reshape(8, 2, 24, 384).transpose(1, 0, 2, 3).reshape(384, 384)
    columns = both[..., 384:].transpose(0, 2, 3, 1, 4).reshape(48, 768)
    own_w = gather(by_y, "x", 4)
    out_by_x, own_w = lax.optimization_barrier((gather_x(columns), own_w))
    other_w = other_core(own_w)
    out_own = lax.all_gather(out_by_x, "y", axis=0, tiled=True)

    core = lax.axis_index("c").reshape(1).astype(jnp.int32)
    blocks = attend(core, lengths, head_temp, whole, own_w, other_w)
    own = lax.all_to_all(blocks, "zl", 0, 0, tiled=True)
    own, out_own = lax.optimization_barrier((own, out_own))
    out_other = other_core(out_own)
    sums = project_half(core, own, out_own)
    return project(core, own, out_other, sums)[None]


def solution(mesh):
    split = Mesh(mesh.devices.reshape(SIZES), AXES)
    clip = ("x", "zh", "y", "c")
    in_specs = (
        P(clip, "zl", None),
        P(),
        P(None, clip, "zl"),
        P("zl", clip),
        P("zl"),
        P(clip),
    )
    out_specs = P(clip, "zl", None)
    return jax.shard_map(
        on_device, mesh=split, in_specs=in_specs, out_specs=out_specs, check_vma=False
    )
```

```python
import functools

import jax
import jax.numpy as jnp
import numpy as np
from jax import lax
from jax.experimental import pallas as pl
from jax.experimental.pallas import tpu as pltpu
from jax.sharding import Mesh, PartitionSpec as P

HD = 64
AXES = ("x", "zh", "y", "c", "zl")
SIZES = (4, 2, 8, 2, 6)


def permute(value, move):
    pairs = []
    for place in np.ndindex(*SIZES):
        goal = move(*place)
        if goal is not None:
            pairs.append(
                (int(np.ravel_multi_index(place, SIZES)), int(np.ravel_multi_index(goal, SIZES)))
            )
    return lax.ppermute(value, AXES, pairs)


def other_core(value):
    return permute(value, lambda x, zh, y, c, zl: (x, zh, y, 1 - c, zl))


def x_swap(value, which):
    goal = {"even": (1, 0, 3, 2), "odd": (3, 2, 1, 0), "across": (2, 3, 0, 1)}[which]
    return permute(value, lambda x, zh, y, c, zl: (goal[x], zh, y, c, zl))


def gather(value, axes, count):
    copies = jnp.broadcast_to(value[None], (count,) + value.shape)
    return lax.all_to_all(copies, axes, 0, 0, tiled=True).reshape(-1, value.shape[1])


def after(value, *others):
    return lax.optimization_barrier((value,) + others)[0]


def gather_x(block):
    x = lax.axis_index("x")
    whole = jnp.zeros((4,) + block.shape, block.dtype)
    for value, at in (
        (block, x),
        (x_swap(block, "even"), x ^ 1),
        (x_swap(block, "odd"), 3 - x),
        (x_swap(block, "across"), (x + 2) % 4),
    ):
        whole = lax.dynamic_update_slice_in_dim(whole, value[None], at, 0)
    return whole.reshape(-1, block.shape[1])


def attend_kernel(core_ref, length_ref, temp_ref, frames, own_w, other_w, *refs):
    out_ref, x_buf, w_buf, qkv, sems = refs
    core = core_ref[0]
    copies = []
    for number in range(4):
        rows = pl.ds(number * 384, 384)
        for source, half in ((own_w, core), (other_w, 1 - core)):
            columns = pl.ds(pl.multiple_of(half * 384, 128), 384)
            copies.append((source.at[rows], w_buf.at[rows, columns]))
    for number in range(6):
        rows = pl.ds(number * 128, 128)
        copies.append((frames.at[rows], x_buf.at[rows]))
    copies = [
        pltpu.make_async_copy(source, goal, sems.at[number])
        for number, (source, goal) in enumerate(copies)
    ]
    for copy in copies:
        copy.start()
    for copy in copies:
        copy.wait()
    qkv[...] = jnp.dot(
        x_buf[...], w_buf[...], preferred_element_type=jnp.float32
    ).astype(jnp.bfloat16)

    total = x_buf.shape[0]
    live = lax.broadcasted_iota(jnp.int32, (total, 1), 0) < length_ref[0]
    lane = lax.broadcasted_iota(jnp.int32, (total, 128), 1)
    place = lax.broadcasted_iota(jnp.int32, (1, 2 * total), 1)
    for two in range(2):
        query, key_part, value = (
            qkv[:, two * 384 + k * 128 : two * 384 + k * 128 + 128] for k in range(3)
        )
        none = jnp.zeros_like(query)
        query = jnp.concatenate(
            [jnp.where(lane < HD, query, none), jnp.where(lane < HD, none, query)]
        )
        scores = lax.dot_general(
            key_part, query, (((1,), (1,)), ((), ())), preferred_element_type=jnp.float32
        )
        scale = jnp.where(place < total, temp_ref[2 * two] / 8.0, temp_ref[2 * two + 1] / 8.0)
        scores = jnp.where(live, scores * scale, -1e30)
        scores = jnp.exp(scores - jnp.max(scores, axis=0, keepdims=True))
        mixed = lax.dot_general(
            value,
            scores.astype(jnp.bfloat16),
            (((0,), (0,)), ((), ())),
            preferred_element_type=jnp.float32,
        )
        mixed = mixed / jnp.sum(scores, axis=0, keepdims=True)
        mixed = jnp.concatenate([mixed[:HD, :total], mixed[HD:, total:]]).T
        out_ref[:, :, two * 128 : two * 128 + 128] = mixed.astype(jnp.bfloat16).reshape(
            out_ref.shape[0], out_ref.shape[1], 128
        )


SMEM = pl.BlockSpec(memory_space=pltpu.SMEM)
VMEM = pl.BlockSpec(memory_space=pltpu.VMEM)
ANYWHERE = pl.BlockSpec(memory_space=pl.ANY)


def attend(core, length, temp, frames, own_w, other_w):
    rows, width = frames.shape
    return pl.pallas_call(
        attend_kernel,
        out_shape=jax.ShapeDtypeStruct((6, rows // 6, 256), jnp.bfloat16),
        in_specs=[SMEM] * 3 + [ANYWHERE] * 3,
        out_specs=VMEM,
        scratch_shapes=[
            pltpu.VMEM((rows, width), jnp.bfloat16),
            pltpu.VMEM((width, 768), jnp.bfloat16),
            pltpu.VMEM((rows, 768), jnp.bfloat16),
            pltpu.SemaphoreType.DMA((14,)),
        ],
        compiler_params=pltpu.CompilerParams(vmem_limit_bytes=50 * 2**20),
        cost_estimate=pl.CostEstimate(
            flops=3 * 10**9, bytes_accessed=5 * 10**6, transcendentals=2 * 10**6
        ),
    )(core, length, temp, frames, own_w, other_w)


def turned_half(heads_ref, which):
    first = jnp.concatenate([heads_ref[at, :, :128] for at in range(6)], axis=1)
    second = jnp.concatenate([heads_ref[at, :, 128:] for at in range(6)], axis=1)
    return jnp.where(which == 0, first, second).T


def project_half_kernel(place_ref, heads_ref, own_any, out_ref, own_ref, sems):
    parts = [pl.ds(number * 384, 384) for number in range(4)]
    copies = [
        pltpu.make_async_copy(own_any.at[rows], own_ref.at[rows], sems.at[number])
        for number, rows in enumerate(parts)
    ]
    for copy in copies:
        copy.start()
    mine = turned_half(heads_ref, place_ref[0])
    for copy, rows in zip(copies, parts):
        copy.wait()
        out_ref[rows] = jnp.dot(own_ref[rows], mine, preferred_element_type=jnp.float32)


def project_kernel(place_ref, heads_ref, other_ref, sums_ref, out_ref, total):
    given = turned_half(heads_ref, 1 - place_ref[0])
    total[...] = sums_ref[...] + jnp.dot(
        other_ref[...], given, preferred_element_type=jnp.float32
    )
    for x in range(4):
        pieces = []
        for zh in range(2):
            for y in range(8):
                at = ((y * 4 + x) * 2 + zh) * 24
                pieces.append(total[at : at + 24, :])
        block = jnp.concatenate(pieces).T
        out_ref[:, x * 384 : x * 384 + 384] = block.astype(jnp.bfloat16)


def project_half(place, heads, own):
    return pl.pallas_call(
        project_half_kernel,
        out_shape=jax.ShapeDtypeStruct((own.shape[0], heads.shape[1]), jnp.float32),
        in_specs=[SMEM, VMEM, ANYWHERE],
        out_specs=VMEM,
        scratch_shapes=[pltpu.VMEM(own.shape, jnp.bfloat16), pltpu.SemaphoreType.DMA((4,))],
        compiler_params=pltpu.CompilerParams(vmem_limit_bytes=16 * 2**20),
        cost_estimate=pl.CostEstimate(
            flops=3 * 10**8, bytes_accessed=3 * 10**6, transcendentals=0
        ),
    )(place, heads, own)


def project(place, heads, other, sums):
    return pl.pallas_call(
        project_kernel,
        out_shape=jax.ShapeDtypeStruct((heads.shape[1], 1536), jnp.bfloat16),
        in_specs=[SMEM] + [VMEM] * 3,
        out_specs=VMEM,
        scratch_shapes=[pltpu.VMEM(sums.shape, jnp.float32)],
        compiler_params=pltpu.CompilerParams(vmem_limit_bytes=16 * 2**20),
        cost_estimate=pl.CostEstimate(
            flops=3 * 10**8, bytes_accessed=4 * 10**6, transcendentals=0
        ),
    )(place, heads, other, sums)


def normalise_kernel(frames_ref, gain_ref, out_ref):
    values = frames_ref[...].astype(jnp.float32)
    rms = jnp.sqrt(jnp.mean(values * values, axis=-1, keepdims=True) + 1e-06)
    out_ref[...] = (values / rms * gain_ref[...]).astype(jnp.bfloat16)


def normalise(frames, gain):
    return pl.pallas_call(
        normalise_kernel,
        out_shape=jax.ShapeDtypeStruct(frames.shape, jnp.bfloat16),
        in_specs=[VMEM] * 2,
        out_specs=VMEM,
        compiler_params=pltpu.CompilerParams(vmem_limit_bytes=58 * 2**20),
        cost_estimate=pl.CostEstimate(
            flops=10**6, bytes_accessed=8 * 10**5, transcendentals=0
        ),
    )(frames, gain[None])


def on_device(latents, norm_gain, w_qkv, w_out, head_temp, lengths):
    normed = normalise(latents[0], norm_gain)
    whole = lax.all_gather(normed, "zl", axis=0, tiled=True)

    rows = w_qkv.reshape(3, 12, 2, 128).transpose(2, 1, 0, 3).reshape(2, 12, 384)
    columns = w_out.T.reshape(12, 2, 128).transpose(1, 0, 2)
    both = jnp.concatenate([rows, columns], axis=2).reshape(1, 2, 48, 128)
    both = jnp.broadcast_to(both, (12, 2, 48, 128)).reshape(24, 48, 128)
    both = lax.all_to_all(after(both, normed), ("zh", "zl", "c"), 0, 0, tiled=True)
    both = both.reshape(2, 6, 2, 12, 512)
    rows = lax.dynamic_index_in_dim(both[..., :384], lax.axis_index("zl"), 1, keepdims=False)
    rows = rows.reshape(48, 384)
    by_y = gather(rows, "y", 8).reshape(8, 2, 24, 384).transpose(1, 0, 2, 3).reshape(384, 384)
    columns = both[..., 384:].transpose(0, 2, 3, 1, 4).reshape(48, 768)
    own_w = gather(by_y, "x", 4)
    out_by_x, own_w = lax.optimization_barrier((gather_x(columns), own_w))
    other_w = other_core(own_w)
    out_own = lax.all_gather(out_by_x, "y", axis=0, tiled=True)

    core = lax.axis_index("c").reshape(1).astype(jnp.int32)
    blocks = attend(core, lengths, head_temp, whole, own_w, other_w)
    own = lax.all_to_all(blocks, "zl", 0, 0, tiled=True)
    own, out_own = lax.optimization_barrier((own, out_own))
    out_other = other_core(out_own)
    sums = project_half(core, own, out_own)
    return project(core, own, out_other, sums)[None]


def solution(mesh):
    split = Mesh(mesh.devices.reshape(SIZES), AXES)
    clip = ("x", "zh", "y", "c")
    in_specs = (
        P(clip, "zl", None),
        P(),
        P(None, clip, "zl"),
        P("zl", clip),
        P("zl"),
        P(clip),
    )
    out_specs = P(clip, "zl", None)
    return jax.shard_map(
        on_device, mesh=split, in_specs=in_specs, out_specs=out_specs, check_vma=False
    )
```
